128 devices in a mesh: expert: 32 (over y, z, core), tensor: 4 (over x).
Axes of the slice: x: 4, y: 4, z: 4, core: 2. Of those that a mesh axis runs over, the one named last changes fastest.
Arguments:
- tokens: bfloat16 [4096, 2560], P('expert', 'tensor'), may hold values from -6 to 6
- cotangent: bfloat16 [4096, 2560], P('expert', 'tensor'), may hold values from -6 to 6
- expert_ids: int32 [4096, 2], P('expert'), may hold values from 0 to 7, all different within a row
- gate_probs: float32 [4096, 2], P('expert'), may hold values from 0.2 to 1
- w_gate: bfloat16 [2560, 81920], P(None, ('expert', 'tensor')), may hold values from -0.125 to 0.125
- w_up: bfloat16 [2560, 81920], P(None, ('expert', 'tensor')), may hold values from -0.125 to 0.125
- w_down: bfloat16 [81920, 2560], P(('expert', 'tensor')), may hold values from -0.0625 to 0.0625
Outputs:
- mixed: bfloat16 [4096, 2560], P('expert', 'tensor')
- token_grad: bfloat16 [4096, 2560], P('expert', 'tensor')
The draws below stay inside these ranges and needn't reach their ends.
Inputs may be any that keep to these rules, and one draw needn't show every extreme that they name: `expert_ids`: each token names 2 different experts, and every expert is named by some token.
All inputs are finite; a program needn't handle non-finite values.
Results may differ from the reference program's by a relative error of at most 0.014.
Values may be sent and summed in bfloat16 or wider, within the bound.
No kernel may reach another device: no remote copies, remote signals or barrier semaphores. Data moves between devices by JAX's collectives and lax.ppermute only.
A program may use at most 128 MiB of HBM per device.

```python
import jax
import jax.numpy as jnp
from jax import lax

D = 2560
FF = 10240
TOP = 2
TOK_DEV = 128
EXPERTS = 8
CAP = 40
BLOCKS = 16
HID = 640
TOKENS = 4096
N_EXPERT = 32


def steps_of(key, dims, split, smallest, top_value):
    def one(dim, blocks):
        draws = jax.random.uniform(jax.random.fold_in(jax.random.fold_in(key, 6), dim), (blocks,), jnp.float32, smallest / len(split), top_value / len(split))
        return jnp.repeat(jnp.exp(draws), dims[dim] // blocks).reshape((-1,) + (1,) * (len(dims) - dim - 1))

    level = one(*split[0])
    for cut in split[1:]:
        level = level * one(*cut)
    return level


def distinct(key, rows, count, top, lift):
    sequence = jax.random.permutation(jax.random.fold_in(key, 1), count)
    boost = sequence
    for power in range(3):
        boost = boost * boost // count
    boost = boost * lift // count
    lots = jax.random.randint(jax.random.fold_in(key, 2), (rows, count), 0, 4096) + boost
    fixed_rows = jax.random.permutation(jax.random.fold_in(key, 3), rows)[jnp.arange(count) % rows]
    lots = jnp.where(jnp.arange(rows)[:, None] == fixed_rows[None, :], 1 << 14, lots)
    merit = lots * count + jnp.arange(count)
    return lax.top_k(merit.astype(jnp.int32), top)[1].astype(jnp.int32)


def bell_draw(key, extent, scale, bound, shards=(), kind=jnp.bfloat16):
    entries = scale * jax.random.normal(key, extent, jnp.float32)
    if shards:
        entries = entries * steps_of(key, extent, shards, -0.22, 0.18)
    return jnp.clip(entries, -bound, bound).astype(kind)


def setup_inputs(seed: int = 0) -> dict:
    streams_of = jax.random.split(jax.random.key(seed), 8)
    tokens = bell_draw(streams_of[0], (TOKENS, D), 1.0, 6.0, ((0, 32), (1, 4)))
    cotangent = bell_draw(streams_of[1], (TOKENS, D), 1.0, 6.0, ((0, 32), (1, 4)))
    expert_ids = distinct(streams_of[2], TOKENS, EXPERTS, TOP, 2048)
    gate_probs = jnp.clip(0.2 + 0.8 * jax.random.uniform(streams_of[3], (TOKENS, TOP), jnp.float32) ** steps_of(streams_of[3], (TOKENS, TOP), ((0, 32),), -0.2, 0.2), 0.2, 1.0)
    w_gate = bell_draw(streams_of[4], (D, EXPERTS * FF), D ** -0.5, 0.125, ((1, 128),))
    w_up = bell_draw(streams_of[5], (D, EXPERTS * FF), D ** -0.5, 0.125, ((1, 128),))
    w_down = bell_draw(streams_of[6], (EXPERTS * FF, D), FF ** -0.5, 0.0625, ((0, 128),))
    return dict(tokens=tokens, cotangent=cotangent, expert_ids=expert_ids, gate_probs=gate_probs, w_gate=w_gate, w_up=w_up, w_down=w_down)


def gelu_tanh(inputs):
    return jax.nn.gelu(inputs, approximate=True)

def reference(tokens, cotangent, expert_ids, gate_probs, w_gate, w_up, w_down):
    assign = TOP * TOK_DEV
    rows_all = N_EXPERT * CAP
    blocks = expert_ids.reshape(N_EXPERT, TOK_DEV, TOP).transpose(0, 2, 1).reshape(N_EXPERT, assign)
    weights = gate_probs.reshape(N_EXPERT, TOK_DEV, TOP).transpose(0, 2, 1).reshape(N_EXPERT, assign)
    expert_range = jnp.arange(EXPERTS, dtype=jnp.int32)
    onehot = (blocks[:, :, None] == expert_range[None, None, :]).astype(jnp.int32)
    before = jnp.cumsum(onehot, axis=1) - onehot
    slot_ids = lax.optimization_barrier(jnp.sum(before * onehot, axis=2))
    kept_mask = slot_ids < CAP
    source = jnp.arange(N_EXPERT, dtype=jnp.int32)[:, None]
    dropped_row = EXPERTS * rows_all
    target = jnp.where(kept_mask, blocks * rows_all + source * CAP + slot_ids, dropped_row)
    assign_ids = jnp.arange(N_EXPERT * assign, dtype=jnp.int32)
    slot_table = jnp.full((dropped_row + 1,), N_EXPERT * assign, jnp.int32)
    slot_table = slot_table.at[target.reshape(-1)].set(assign_ids)[:-1].reshape(EXPERTS, rows_all)
    token_of = (source * TOK_DEV + (jnp.arange(assign, dtype=jnp.int32) % TOK_DEV)[None, :]).reshape(-1)
    token_pad = jnp.concatenate([tokens[token_of], jnp.zeros((1, D), jnp.bfloat16)], axis=0)
    scaled = (weights.reshape(-1)[:, None] * cotangent[token_of].astype(jnp.float32)).astype(jnp.bfloat16)
    scaled_pad = jnp.concatenate([scaled, jnp.zeros((1, D), jnp.bfloat16)], axis=0)

    def expert_pass(expert_index):
        row_ids = slot_table[expert_index]
        token_rows = token_pad[row_ids]
        scaled_rows = scaled_pad[row_ids]
        gate_cols = lax.dynamic_slice_in_dim(w_gate, expert_index * FF, FF, 1)
        up_cols = lax.dynamic_slice_in_dim(w_up, expert_index * FF, FF, 1)
        down_rows = lax.dynamic_slice_in_dim(w_down, expert_index * FF, FF, 0)
        gate_pre = jnp.dot(token_rows, gate_cols, preferred_element_type=jnp.float32)
        up_pre = jnp.dot(token_rows, up_cols, preferred_element_type=jnp.float32)
        back_act = jnp.dot(scaled_rows, down_rows.T, preferred_element_type=jnp.float32)
        gelu_val, gelu_back = jax.vjp(gelu_tanh, gate_pre)
        activation = (gelu_val * up_pre).astype(jnp.bfloat16)
        grad_gate = gelu_back(back_act * up_pre)[0].astype(jnp.bfloat16)
        grad_up = (back_act * gelu_val).astype(jnp.bfloat16)

        def add_block(block_index, totals):
            offset = block_index * HID
            act_part = lax.dynamic_slice_in_dim(activation, offset, HID, 1)
            gate_part = lax.dynamic_slice_in_dim(grad_gate, offset, HID, 1)
            up_part = lax.dynamic_slice_in_dim(grad_up, offset, HID, 1)
            down_part = lax.dynamic_slice_in_dim(down_rows, offset, HID, 0)
            gcol_part = lax.dynamic_slice_in_dim(gate_cols, offset, HID, 1)
            ucol_part = lax.dynamic_slice_in_dim(up_cols, offset, HID, 1)
            out_block = jnp.dot(act_part, down_part, preferred_element_type=jnp.float32).astype(jnp.bfloat16)
            grad_block = (jnp.dot(gate_part, gcol_part.T, preferred_element_type=jnp.float32) + jnp.dot(up_part, ucol_part.T, preferred_element_type=jnp.float32)).astype(jnp.bfloat16)
            out_block, grad_block = lax.optimization_barrier((out_block, grad_block))
            return (totals[0] + out_block.astype(jnp.float32), totals[1] + grad_block.astype(jnp.float32))
        zero_rows = jnp.zeros((rows_all, D), jnp.float32)
        return lax.fori_loop(0, BLOCKS, add_block, (zero_rows, zero_rows))
    expert_out, expert_dx = lax.map(expert_pass, expert_range)
    pad_row = jnp.zeros((1, D), jnp.float32)
    flat_out = jnp.concatenate([expert_out.reshape(dropped_row, D), pad_row], axis=0)
    flat_dx = jnp.concatenate([expert_dx.reshape(dropped_row, D), pad_row], axis=0)
    position = target.reshape(N_EXPERT, TOP, TOK_DEV)
    gates = weights.reshape(N_EXPERT, TOP, TOK_DEV)
    out_add = lax.optimization_barrier(jnp.sum(gates[..., None] * flat_out[position], axis=1)).reshape(TOKENS, D)
    grad_add = lax.optimization_barrier(jnp.sum(flat_dx[position], axis=1)).reshape(TOKENS, D)
    mixed = (tokens.astype(jnp.float32) + out_add).astype(jnp.bfloat16)
    token_grad = (cotangent.astype(jnp.float32) + grad_add).astype(jnp.bfloat16)
    return (mixed, token_grad)
```

```python
import functools

import jax
import jax.numpy as jnp
from jax import lax
from jax.experimental import pallas as pl
from jax.experimental.pallas import tpu as pltpu
from jax.sharding import Mesh, PartitionSpec as P

F32 = jnp.float32
BF16 = jnp.bfloat16
CONTRACT_LAST = (((1,), (1,)), ((), ()))
HIDDEN_TILE = 256


def geglu(gate, up, back):
    root = 0.7978845608028654
    cubic = 0.044715
    square = gate * gate
    tanh = jnp.tanh(gate * (root + root * cubic * square))
    half = 0.5 * (1.0 + tanh)
    value = gate * half
    slope = half + 0.5 * gate * (1.0 - tanh * tanh) * (root + 3.0 * root * cubic * square)
    return (
        (value * up).astype(BF16),
        (slope * (back * up)).astype(BF16),
        (value * back).astype(BF16),
    )


def experts_body(
    rows,
    gate_a,
    up_a,
    down_a,
    gate_b,
    up_b,
    down_b,
    sums,
    tok,
    sca,
    w_gate,
    w_up,
    w_down,
    act,
    grad_gate,
    grad_up,
    stage,
    in_sem,
    out_sem,
):
    spans, width = rows.shape[1], rows.shape[3]
    hidden = gate_a.shape[1]
    tile = HIDDEN_TILE
    copies = []

    def fetch(src, dst):
        copy = pltpu.make_async_copy(src, dst, in_sem.at[len(copies)])
        copy.start()
        copies.append(copy)

    for x in range(spans):
        fetch(rows.at[0, x], tok.at[:, pl.ds(x * width, width)])
    fetch(gate_a, w_gate.at[:, pl.ds(0, hidden)])
    fetch(up_a, w_up.at[:, pl.ds(0, hidden)])
    for x in range(spans):
        fetch(rows.at[1, x], sca.at[:, pl.ds(x * width, width)])
    fetch(down_a, w_down.at[pl.ds(0, hidden), :])
    first = len(copies)
    fetch(gate_b, w_gate.at[:, pl.ds(hidden, hidden)])
    fetch(up_b, w_up.at[:, pl.ds(hidden, hidden)])
    fetch(down_b, w_down.at[pl.ds(hidden, hidden), :])

    def hidden_tile(i, carry):
        at = pl.ds(pl.multiple_of(i * tile, tile), tile)
        gate = jnp.dot(tok[...], w_gate[:, at], preferred_element_type=F32)
        up = jnp.dot(tok[...], w_up[:, at], preferred_element_type=F32)
        back = lax.dot_general(sca[...], w_down[at, :], CONTRACT_LAST, preferred_element_type=F32)
        act[:, at], grad_gate[:, at], grad_up[:, at] = geglu(gate, up, back)
        return carry

    for copy in copies[:first]:
        copy.wait()
    lax.fori_loop(0, hidden // tile, hidden_tile, 0)
    for copy in copies[first:]:
        copy.wait()
    lax.fori_loop(hidden // tile, 2 * hidden // tile, hidden_tile, 0)

    sends = []
    for x in range(spans):
        at = pl.ds(x * width, width)
        stage[0, x] = jnp.dot(act[...], w_down[:, at], preferred_element_type=F32).astype(BF16)
        total = lax.dot_general(
            grad_gate[...], w_gate[at, :], CONTRACT_LAST, preferred_element_type=F32
        )
        total += lax.dot_general(
            grad_up[...], w_up[at, :], CONTRACT_LAST, preferred_element_type=F32
        )
        stage[1, x] = total.astype(BF16)
        for kind in range(2):
            send = pltpu.make_async_copy(
                stage.at[kind, x], sums.at[kind, x], out_sem.at[2 * x + kind]
            )
            send.start()
            sends.append(send)
    for send in sends:
        send.wait()


def experts(rows, mine, other):
    _, spans, count, width = rows.shape
    model = spans * width
    hidden = mine[0].shape[1]
    return pl.pallas_call(
        experts_body,
        out_shape=jax.ShapeDtypeStruct(rows.shape, BF16),
        in_specs=[pl.BlockSpec(memory_space=pl.ANY)] * 7,
        out_specs=pl.BlockSpec(memory_space=pl.ANY),
        scratch_shapes=[
            pltpu.VMEM((count, model), BF16),
            pltpu.VMEM((count, model), BF16),
            pltpu.VMEM((model, 2 * hidden), BF16),
            pltpu.VMEM((model, 2 * hidden), BF16),
            pltpu.VMEM((2 * hidden, model), BF16),
            pltpu.VMEM((count, 2 * hidden), BF16),
            pltpu.VMEM((count, 2 * hidden), BF16),
            pltpu.VMEM((count, 2 * hidden), BF16),
            pltpu.VMEM(rows.shape, BF16),
            pltpu.SemaphoreType.DMA((2 * spans + 6,)),
            pltpu.SemaphoreType.DMA((2 * spans,)),
        ],
        compiler_params=pltpu.CompilerParams(vmem_limit_bytes=56 * 2**20),
        cost_estimate=pl.CostEstimate(
            flops=24 * count * model * hidden,
            bytes_accessed=8 * count * model + 12 * model * hidden,
            transcendentals=2 * count * hidden,
        ),
        name="experts",
    )(rows, *mine, *other)


def shards(tokens, cotangent, expert_ids, gate_probs, w_gate, w_up, w_down):
    n_experts = lax.axis_size("e")
    count, top = expert_ids.shape
    width = tokens.shape[1]
    capacity = (5 * count * top + 4 * n_experts - 1) // (4 * n_experts)
    spans = lax.axis_size("x")
    slots = n_experts * capacity

    mine = (w_gate, w_up, w_down)
    other = tuple(lax.ppermute(w, "c", [(0, 1), (1, 0)]) for w in mine)

    flat_ids = expert_ids.T.reshape(-1)
    onehot = (flat_ids[:, None] == jnp.arange(n_experts, dtype=jnp.int32)[None, :]).astype(
        jnp.int32
    )
    before = jnp.cumsum(onehot, axis=0) - onehot
    slot_ids = jnp.sum(before * onehot, axis=1)
    position = jnp.where(slot_ids < capacity, flat_ids * capacity + slot_ids, slots)
    hit = jnp.arange(slots, dtype=jnp.int32)[:, None] == position[None, :]
    pick = [hit[:, k * count : (k + 1) * count] for k in range(top)]
    any_pick = functools.reduce(jnp.logical_or, pick).astype(BF16)
    row_gate = jnp.sum(jnp.where(hit, gate_probs.T.reshape(-1)[None, :], 0.0), axis=1)
    token_rows = jnp.dot(any_pick, tokens, preferred_element_type=F32).astype(BF16)
    scaled_rows = (
        jnp.dot(any_pick, cotangent, preferred_element_type=F32) * row_gate[:, None]
    ).astype(BF16)

    shape = (n_experts, 1, capacity, width)
    send = jnp.concatenate([token_rows.reshape(shape), scaled_rows.reshape(shape)], axis=1)
    send = send.reshape(2 * n_experts, capacity, width)
    mine_rows = lax.all_to_all(send, ("e", "z"), split_axis=0, concat_axis=0, tiled=True)
    n_rows = 2 * slots
    rows = lax.all_gather(mine_rows.reshape(n_rows, width), ("z", "x"), axis=0, tiled=False)
    rows = rows.reshape(2, spans, n_rows, width)

    sums = experts(rows, mine, other)

    total = lax.psum_scatter(
        sums.reshape(2 * spans, n_rows, width), ("z", "x"), scatter_dimension=0, tiled=True
    )
    back = lax.all_to_all(
        total.reshape(2 * n_experts, capacity, width),
        ("e", "z"),
        split_axis=0,
        concat_axis=0,
        tiled=True,
    ).reshape(n_experts, 2, capacity, width)
    out_rows = back[:, 0].reshape(slots, width)
    grad_rows = back[:, 1].reshape(slots, width)

    out_add = 0.0
    for k in range(top):
        picked = lax.dot_general(
            pick[k].astype(BF16),
            out_rows,
            (((0,), (0,)), ((), ())),
            preferred_element_type=F32,
        )
        out_add = out_add + gate_probs[:, k : k + 1] * picked
    grad_add = lax.dot_general(
        any_pick, grad_rows, (((0,), (0,)), ((), ())), preferred_element_type=F32
    )
    mixed = (tokens.astype(F32) + out_add).astype(BF16)
    token_grad = (cotangent.astype(F32) + grad_add).astype(BF16)
    return (mixed, token_grad)


def solution(mesh):
    n_expert, n_tensor = mesh.devices.shape
    fine = Mesh(mesh.devices.reshape(n_expert // 4, 2, 2, n_tensor), ("e", "z", "c", "x"))
    shard = ("e", "z", "c")
    everywhere = ("e", "z", "c", "x")
    placed = (
        P(shard, "x"),
        P(shard, "x"),
        P(shard, None),
        P(shard, None),
        P(None, everywhere),
        P(None, everywhere),
        P(everywhere, None),
    )
    return jax.shard_map(
        shards,
        mesh=fine,
        in_specs=placed,
        out_specs=(P(shard, "x"), P(shard, "x")),
        check_vma=False,
    )
```

```python
import functools

import jax
import jax.numpy as jnp
from jax import lax
from jax.experimental import pallas as pl
from jax.experimental.pallas import tpu as pltpu
from jax.sharding import Mesh, PartitionSpec as P

F32 = jnp.float32
BF16 = jnp.bfloat16
CONTRACT_LAST = (((1,), (1,)), ((), ()))
HIDDEN_TILE = 256
VMEM_MB = 56
FIRST_KS = (2, 3)
LAST_KS = (1, 0)


def geglu(gate, up, back):
    root = 0.7978845608028654
    cubic = 0.044715
    square = gate * gate
    tanh = jnp.tanh(gate * (root + root * cubic * square))
    half = 0.5 * (1.0 + tanh)
    value = gate * half
    slope = half + 0.5 * gate * (1.0 - tanh * tanh) * (root + 3.0 * root * cubic * square)
    return (
        (value * up).astype(BF16),
        (slope * (back * up)).astype(BF16),
        (value * back).astype(BF16),
    )


def fetcher(sems):
    copies = []

    def fetch(src, dst):
        copy = pltpu.make_async_copy(src, dst, sems.at[len(copies)])
        copy.start()
        copies.append(copy)
        return copy

    return fetch, copies


def columns(place, k, width):
    spans = 4
    span = lax.rem(place[1] + place[2] * k + 2 * spans, spans)
    return pl.ds(pl.multiple_of(span * width, 128), width)


def fetch_parts(place, parts, near, both, fetch):
    rows, width = parts[0].shape
    for piece, row, count, kind, k, to in held(rows, near):
        fetch(
            parts[piece].at[pl.ds(row, count)],
            both.at[lax.rem(place[0] + kind, 2), pl.ds(to, count), columns(place, k, width)],
        )


def front(both, weights, acts, row, hidden, waits):
    w_gate, w_up, w_down = weights
    tile = HIDDEN_TILE
    rows = pl.ds(row, both.shape[1])

    def hidden_tile(i, carry):
        at = pl.ds(pl.multiple_of(i * tile, tile), tile)
        gate = jnp.dot(both[0], w_gate[:, at], preferred_element_type=F32)
        up = jnp.dot(both[0], w_up[:, at], preferred_element_type=F32)
        back = lax.dot_general(both[1], w_down[at, :], CONTRACT_LAST, preferred_element_type=F32)
        for ref, value in zip(acts, geglu(gate, up, back)):
            ref[rows, at] = value
        return carry

    waits[0]()
    lax.fori_loop(0, hidden // tile, hidden_tile, 0)
    waits[1]()
    lax.fori_loop(hidden // tile, 2 * hidden // tile, hidden_tile, 0)


def back_products(acts, down, gate_rows, up_rows):
    act, grad_gate, grad_up = acts
    out = jnp.dot(act[...], down, preferred_element_type=F32)
    total = lax.dot_general(
        grad_gate[...], gate_rows, CONTRACT_LAST, preferred_element_type=F32
    )
    total += lax.dot_general(grad_up[...], up_rows, CONTRACT_LAST, preferred_element_type=F32)
    return out.astype(BF16), total.astype(BF16)


def send_piece(place, stage, j, values, near_outs, far_outs, send):
    for kind, value in enumerate(values):
        stage[lax.rem(place[0] + kind, 2), j] = value
    row = 0
    for out in near_outs:
        send(stage.at[:, j, pl.ds(row, out.shape[1])], out)
        row += out.shape[1]
    for kind in range(2):
        send(stage.at[kind, j, pl.ds(row, far_outs[kind].shape[1])], far_outs[kind].at[j])


def outs_of(ks, near, far, width):
    shapes = []
    for k in ks:
        shapes += [shaped(2, near // 2, width)] * 2 if k else [shaped(2, near, width)]
    return shapes + [shaped(len(ks), far, width)] * 2


def by_span(ks, outs):
    spans, at = [], 0
    for k in ks:
        spans.append(outs[at : at + (2 if k else 1)])
        at += len(spans[-1])
    return spans, outs[at:]


def load_weights(given, held, hidden, fetch):
    for half in range(2):
        at = pl.ds(half * hidden, hidden)
        gate, up, down = given[3 * half : 3 * half + 3]
        fetch(gate, held[0].at[:, at])
        fetch(up, held[1].at[:, at])
        fetch(down, held[2].at[at, :])


def waiter(copies):
    def wait():
        for copy in copies:
            copy.wait()

    return wait


def middle_body(first_ks, near, place, *refs):
    n_in = 10
    parts, given, outs = refs[:n_in], refs[n_in : n_in + 6], refs[n_in + 6 : -10]
    both, w_gate, w_up, w_down, act, grad_gate, grad_up, stage, in_sem, out_sem = refs[-10:]
    hidden, width = given[0].shape[1], parts[0].shape[1]
    acts = (act, grad_gate, grad_up)
    fetch, copies = fetcher(in_sem)
    fetch_parts(place, parts, near, both, fetch)
    n = len(copies)
    load_weights(given, (w_gate, w_up, w_down), hidden, fetch)
    waits = (waiter(copies[: n + 3]), waiter(copies[n + 3 :]))
    front(both, (w_gate, w_up, w_down), acts, 0, hidden, waits)
    send, sends = fetcher(out_sem)
    for ref, out in zip(acts, outs[:3]):
        send(ref, out)
    spans, far_outs = by_span(first_ks, outs[3:])
    for j, k in enumerate(first_ks):
        at = columns(place, k, width)
        values = back_products(acts, w_down[:, at], w_gate[at, :], w_up[at, :])
        send_piece(place, stage, j, values, spans[j], far_outs, send)
    waiter(sends)()


def last_body(last_ks, place, *refs):
    given, done, outs = refs[:6], refs[6:9], refs[9:-9]
    down, gate_rows, up_rows, act, grad_gate, grad_up, stage, in_sem, out_sem = refs[-9:]
    hidden, width = given[0].shape[1], stage.shape[3]
    acts = (act, grad_gate, grad_up)
    fetch, copies = fetcher(in_sem)

    def load(j, k):
        at = columns(place, k, width)
        for half in range(2):
            mine = pl.ds(half * hidden, hidden)
            gate, up, dn = given[3 * half : 3 * half + 3]
            fetch(dn.at[:, at], down.at[j, mine, :])
            fetch(gate.at[at, :], gate_rows.at[j, :, mine])
            fetch(up.at[at, :], up_rows.at[j, :, mine])

    load(0, last_ks[0])
    for ref, dst in zip(done, acts):
        fetch(ref, dst)
    for j, k in enumerate(last_ks[1:]):
        load(j + 1, k)
    send, sends = fetcher(out_sem)
    spans, far_outs = by_span(last_ks, outs)
    for j in range(len(last_ks)):
        waiter(copies[0:9] if j == 0 else copies[3 + 6 * j : 9 + 6 * j])()
        values = back_products(acts, down[j], gate_rows[j], up_rows[j])
        send_piece(place, stage, j, values, spans[j], far_outs, send)
    waiter(sends)()


def call(body, name, out_shape, scratch, flops, operands):
    n_bytes = sum(o.size * o.dtype.itemsize for o in operands)
    n_bytes += sum(2 * o.size for o in out_shape)
    return pl.pallas_call(
        body,
        out_shape=out_shape,
        in_specs=[pl.BlockSpec(memory_space=pltpu.SMEM)]
        + [pl.BlockSpec(memory_space=pl.ANY)] * (len(operands) - 1),
        out_specs=[pl.BlockSpec(memory_space=pl.ANY)] * len(out_shape),
        scratch_shapes=scratch,
        compiler_params=pltpu.CompilerParams(vmem_limit_bytes=VMEM_MB * 2**20),
        cost_estimate=pl.CostEstimate(flops=flops, bytes_accessed=n_bytes, transcendentals=0),
        name=name,
    )(*operands)


def shaped(*shape):
    return jax.ShapeDtypeStruct(shape, BF16)


def held_weights(model, hidden):
    return [
        pltpu.VMEM((model, 2 * hidden), BF16),
        pltpu.VMEM((model, 2 * hidden), BF16),
        pltpu.VMEM((2 * hidden, model), BF16),
    ]


def middle_call(place, parts, near, weights):
    rows, width = parts[0].shape
    model, hidden = weights[0].shape
    n = len(FIRST_KS)
    outs = call(
        functools.partial(middle_body, FIRST_KS, near),
        "middle",
        [shaped(rows, 2 * hidden)] * 3 + outs_of(FIRST_KS, near, rows - near, width),
        [pltpu.VMEM((2, rows, model), BF16)]
        + held_weights(model, hidden)
        + [pltpu.VMEM((rows, 2 * hidden), BF16)] * 3
        + [pltpu.VMEM((2, n, rows, width), BF16)]
        + [pltpu.SemaphoreType.DMA((19,)), pltpu.SemaphoreType.DMA((3 + 4 * n,))],
        12 * rows * model * hidden + 12 * n * rows * width * hidden,
        (place, *parts, *weights),
    )
    return outs[:3], by_span(FIRST_KS, outs[3:])


def last_call(place, weights, done, near):
    rows = done[0].shape[0]
    model, hidden = weights[0].shape
    width = model // 4
    n = len(LAST_KS)
    outs = call(
        functools.partial(last_body, LAST_KS),
        "last",
        outs_of(LAST_KS, near, rows - near, width),
        [
            pltpu.VMEM((n, 2 * hidden, width), BF16),
            pltpu.VMEM((n, width, 2 * hidden), BF16),
            pltpu.VMEM((n, width, 2 * hidden), BF16),
        ]
        + [pltpu.VMEM((rows, 2 * hidden), BF16)] * 3
        + [pltpu.VMEM((2, n, rows, width), BF16)]
        + [pltpu.SemaphoreType.DMA((3 + 6 * n,)), pltpu.SemaphoreType.DMA((4 * n,))],
        12 * n * rows * width * hidden,
        (place, *weights, *done),
    )
    return by_span(LAST_KS, outs)


def add(*terms):
    return sum(t.astype(F32) for t in terms).astype(BF16)


def turned(step):
    spans = lax.axis_size("x")
    return [
        (c * spans + x, c * spans + (x + (1 - 2 * c) * step) % spans)
        for c in range(2)
        for x in range(spans)
    ]


def ahead(block):
    return lax.ppermute(block, ("c", "x"), turned(1))


def behind(block):
    return lax.ppermute(block, ("c", "x"), turned(-1))


def across(block):
    return lax.ppermute(block, "z", [(0, 1), (1, 0)])


def gather(own, near):
    half, split = near // 2, own.shape[0] // 2
    barrier = lax.optimization_barrier
    partner, a, b = barrier((across(own), ahead(own), behind(own)))
    up = ahead(jnp.concatenate([partner[:near], a[:split]]))
    down = behind(jnp.concatenate([partner[:near], b[split:]]))
    over = across(jnp.concatenate([a[near:], b[near:]]))
    up, down, over = barrier((up, down, over))
    last = (ahead(up[:half]), behind(down[half:near]), across(down[2 * near - split :]))
    return [own, partner, a, b, up, down, over, *last]


def held(rows, near):
    half, split = near // 2, rows // 2
    far = rows - near
    return (
        (0, 0, rows, 0, 0, 0),
        (1, 0, rows, 1, 0, 0),
        (2, 0, rows, 0, 3, 0),
        (3, 0, rows, 0, 1, 0),
        (4, 0, near, 1, 3, 0),
        (4, near, split, 0, 2, 0),
        (5, 0, near, 1, 1, 0),
        (5, near, rows - split, 0, 2, split),
        (6, 0, far, 1, 3, near),
        (6, far, far, 1, 1, near),
        (7, 0, half, 1, 2, 0),
        (8, 0, near - half, 1, 2, half),
        (9, 0, far, 1, 2, near),
    )


def shards(tokens, cotangent, expert_ids, gate_probs, w_gate, w_up, w_down):
    n_experts = lax.axis_size("e")
    count, top = expert_ids.shape
    width = tokens.shape[1]
    capacity = (5 * count * top + 4 * n_experts - 1) // (4 * n_experts)
    slots = n_experts * capacity

    mine = (w_gate, w_up, w_down)
    other = tuple(lax.ppermute(w, "c", [(0, 1), (1, 0)]) for w in mine)
    place = jnp.stack(
        [lax.axis_index("z"), lax.axis_index("x"), 1 - 2 * lax.axis_index("c"), lax.axis_index("c")]
    ).astype(jnp.int32)

    flat_ids = expert_ids.T.reshape(-1)
    onehot = (flat_ids[:, None] == jnp.arange(n_experts, dtype=jnp.int32)[None, :]).astype(
        jnp.int32
    )
    before = jnp.cumsum(onehot, axis=0) - onehot
    slot_ids = jnp.sum(before * onehot, axis=1)
    position = jnp.where(slot_ids < capacity, flat_ids * capacity + slot_ids, slots)
    hit = jnp.arange(slots, dtype=jnp.int32)[:, None] == position[None, :]
    pick = [hit[:, k * count : (k + 1) * count] for k in range(top)]
    any_pick = functools.reduce(jnp.logical_or, pick).astype(BF16)
    row_gate = jnp.sum(jnp.where(hit, gate_probs.T.reshape(-1)[None, :], 0.0), axis=1)
    token_rows = jnp.dot(any_pick, tokens, preferred_element_type=F32).astype(BF16)
    scaled_rows = (
        jnp.dot(any_pick, cotangent, preferred_element_type=F32) * row_gate[:, None]
    ).astype(BF16)

    shape = (n_experts, 1, capacity, width)
    send = jnp.concatenate([token_rows.reshape(shape), scaled_rows.reshape(shape)], axis=1)
    send = send.reshape(2 * n_experts, capacity, width)
    def exchange(block):
        return lax.all_to_all(block, ("e", "z"), split_axis=0, concat_axis=0, tiled=True)

    n_rows = 2 * slots
    near = -(-11 * n_rows // (20 * 32)) * 32
    own, *other = lax.optimization_barrier((exchange(send).reshape(n_rows, width), *other))
    weights = (*mine, *other)
    parts = gather(own, near)
    done, (((two_lo, two_hi), (three_lo, three_hi)), (my_a, their_a)) = middle_call(
        place, parts, near, weights
    )
    two_up, two_down = ahead(two_lo), behind(two_hi)
    got_a, three_down = across(their_a), behind(three_lo)
    (((one_lo, one_hi), (zero,)), (my_b, their_b)) = last_call(place, weights, done, near)
    got_b, one_up = across(their_b), ahead(one_hi)
    rest_up, rest_down = ahead(add(one_lo, two_up)), behind(add(three_hi, two_down))
    half = near // 2
    near_lo = [add(zero[i, :half], rest_up[i], three_down[i]) for i in range(2)]
    near_hi = [add(zero[i, half:], one_up[i], rest_down[i]) for i in range(2)]
    near_total = add(
        jnp.concatenate([near_lo[0], near_hi[0]]),
        across(jnp.concatenate([near_lo[1], near_hi[1]])),
    )
    quarter = (n_rows - near) // 2
    sum_two, sum_three = add(my_a[0], got_a[0]), add(my_a[1], got_a[1])
    sum_one, sum_zero = add(my_b[0], got_b[0]), add(my_b[1], got_b[1])
    far_up = ahead(jnp.concatenate([sum_two[:quarter], sum_one[quarter:]]))
    far_down = behind(jnp.concatenate([sum_three[:quarter], sum_two[quarter:]]))
    far_rest_up = ahead(add(sum_one[:quarter], far_up[:quarter]))
    far_rest_down = behind(add(sum_three[quarter:], far_down[quarter:]))
    far_lo = add(sum_zero[:quarter], far_rest_up, far_down[:quarter])
    far_hi = add(sum_zero[quarter:], far_up[quarter:], far_rest_down)
    total = jnp.concatenate([near_total, far_lo, far_hi])
    back = exchange(total.reshape(2 * n_experts, capacity, width))
    back = back.reshape(n_experts, 2, capacity, width)
    out_rows = back[:, 0].reshape(slots, width)
    grad_rows = back[:, 1].reshape(slots, width)

    out_add = 0.0
    for k in range(top):
        picked = lax.dot_general(
            pick[k].astype(BF16),
            out_rows,
            (((0,), (0,)), ((), ())),
            preferred_element_type=F32,
        )
        out_add = out_add + gate_probs[:, k : k + 1] * picked
    grad_add = lax.dot_general(
        any_pick, grad_rows, (((0,), (0,)), ((), ())), preferred_element_type=F32
    )
    mixed = (tokens.astype(F32) + out_add).astype(BF16)
    token_grad = (cotangent.astype(F32) + grad_add).astype(BF16)
    return (mixed, token_grad)


def solution(mesh):
    n_expert, n_tensor = mesh.devices.shape
    fine = Mesh(mesh.devices.reshape(n_expert // 4, 2, 2, n_tensor), ("e", "z", "c", "x"))
    shard = ("e", "z", "c")
    everywhere = ("e", "z", "c", "x")
    placed = (
        P(shard, "x"),
        P(shard, "x"),
        P(shard, None),
        P(shard, None),
        P(None, everywhere),
        P(None, everywhere),
        P(everywhere, None),
    )
    return jax.shard_map(
        shards,
        mesh=fine,
        in_specs=placed,
        out_specs=(P(shard, "x"), P(shard, "x")),
        check_vma=False,
    )
```

```python
import functools

import jax
import jax.numpy as jnp
from jax import lax
from jax.experimental import pallas as pl
from jax.experimental.pallas import tpu as pltpu
from jax.sharding import Mesh, PartitionSpec as P

F32 = jnp.float32
BF16 = jnp.bfloat16
CONTRACT_LAST = (((1,), (1,)), ((), ()))
HIDDEN_TILE = 256
VMEM_MB = dict(front=8, middle=16, last=10)
OUT_ORDER = (2, 1, 3, 0)
FAR_SHARE = (16, 20)
GRAD_ORDER = (2, 1)
LAST_ORDER = (3, 0)


def geglu(gate, up, back):
    root = 0.7978845608028654
    cubic = 0.044715
    square = gate * gate
    tanh = jnp.tanh(gate * (root + root * cubic * square))
    half = 0.5 * (1.0 + tanh)
    value = gate * half
    slope = half + 0.5 * gate * (1.0 - tanh * tanh) * (root + 3.0 * root * cubic * square)
    return (
        (value * up).astype(BF16),
        (slope * (back * up)).astype(BF16),
        (value * back).astype(BF16),
    )


def fetcher(sems):
    copies = []

    def fetch(src, dst):
        copy = pltpu.make_async_copy(src, dst, sems.at[len(copies)])
        copy.start()
        copies.append(copy)
        return copy

    return fetch, copies


def columns(place, k, width):
    spans = 4
    span = lax.rem(place[1] + place[2] * k + 2 * spans, spans)
    return pl.ds(pl.multiple_of(span * width, 128), width)


def fetch_rows(place, pieces, dst, fetch):
    return [
        fetch(
            ref.at[pl.ds(row, count)],
            dst.at[pl.ds(to, count), columns(place, k, ref.shape[1])],
        )
        for ref, row, count, k, to in pieces
    ]


def front(tok, sca, weights, acts, row, waits):
    w_gate, w_up, w_down = weights
    tile = HIDDEN_TILE
    rows = pl.ds(row, tok.shape[0])

    def hidden_tile(i, carry):
        at = pl.ds(pl.multiple_of(i * tile, tile), tile)
        gate = jnp.dot(tok[...], w_gate[:, at], preferred_element_type=F32)
        up = jnp.dot(tok[...], w_up[:, at], preferred_element_type=F32)
        back = lax.dot_general(sca[...], w_down[at, :], CONTRACT_LAST, preferred_element_type=F32)
        for ref, value in zip(acts, geglu(gate, up, back)):
            ref[rows, at] = value
        return carry

    for wait in waits:
        wait()
    lax.fori_loop(0, w_gate.shape[1] // tile, hidden_tile, 0)


def grad_product(grads, gate_rows, up_rows):
    total = lax.dot_general(
        grads[0][...], gate_rows, CONTRACT_LAST, preferred_element_type=F32
    )
    total += lax.dot_general(grads[1][...], up_rows, CONTRACT_LAST, preferred_element_type=F32)
    return total.astype(BF16)


def waiter(copies):
    def wait():
        for copy in copies:
            copy.wait()

    return wait


def front_body(place, *refs):
    own, behind_1, ahead_1, up, down = refs[:5]
    held, outs = refs[5:8], refs[8:11]
    tok, sca, in_sem = refs[11:]
    n = tok.shape[0]
    fetch, _ = fetcher(in_sem)
    toks = [(own, 0, n, 0, 0), (behind_1, 0, n, 3, 0), (ahead_1, 0, n, 1, 0), (up, n, n, 2, 0)]
    scas = [(own, n, n, 0, 0), (behind_1, n, n, 3, 0), (ahead_1, n, n, 1, 0), (down, n, n, 2, 0)]
    copies = fetch_rows(place, toks, tok, fetch) + fetch_rows(place, scas, sca, fetch)
    front(tok, sca, held, outs, 0, [waiter(copies)])


def middle_body(place, *refs):
    partner, up, down, over, last_up, last_down, last_over = refs[:7]
    held, done, outs = refs[7:10], refs[10:13], refs[13:-6]
    w_gate, w_up, w_down = held
    tok, sca, act, grad_gate, grad_up, in_sem = refs[-6:]
    n, width = tok.shape[0], partner.shape[1]
    acts = (act, grad_gate, grad_up)
    fetch, _ = fetcher(in_sem)
    toks = [(partner, 0, n, 0, 0), (up, 0, n, 3, 0), (down, 0, n, 1, 0)]
    toks += [(last_up, 0, n // 2, 2, 0), (last_down, 0, n // 2, 2, n // 2)]
    scas = [(partner, n, n, 0, 0), (over, 0, n, 3, 0), (over, n, n, 1, 0), (last_over, 0, n, 2, 0)]
    copies = fetch_rows(place, toks, tok, fetch) + fetch_rows(place, scas, sca, fetch)
    acts_in = [fetch(ref, dst.at[pl.ds(0, n)]) for ref, dst in zip(done, acts)]
    front(tok, sca, held, acts, n, [waiter(copies)])
    waiter(acts_in)()
    for ref, out in zip(acts[1:], outs[:2]):
        out[...] = ref[pl.ds(n, n), :]
    mine, theirs, up_1, one_lo, two_hi, out_three, out_zero = outs[2:]
    far, h = mine.shape[1], one_lo.shape[1]
    rest = n - h
    for j, k in enumerate(OUT_ORDER):
        at = columns(place, k, width)
        value = jnp.dot(act[...], w_down[:, at], preferred_element_type=F32).astype(BF16)
        mine[j] = value[:far]
        theirs[j] = value[n : n + far]
        tails = value[far:n], value[n + far :]
        for kind in range(2):
            if k == 2:
                two_hi[kind, pl.ds(rest, n - far)] = tails[kind]
            elif k == 1:
                up_1[kind, pl.ds(n, n - far)] = tails[kind]
            else:
                (out_three if k == 3 else out_zero)[kind] = tails[kind]
    for k in GRAD_ORDER:
        at = columns(place, k, width)
        value = grad_product(acts[1:], w_gate[at, :], w_up[at, :])
        for kind in range(2):
            lower, upper = value[kind * n : kind * n + h], value[kind * n + h : (kind + 1) * n]
            if k == 2:
                up_1[kind, pl.ds(0, h)] = lower
                two_hi[kind, pl.ds(0, rest)] = upper
            else:
                up_1[kind, pl.ds(h, rest)] = upper
                one_lo[kind] = lower


def last_body(place, *refs):
    w_gate, w_up, early, late, tails = refs[0], refs[1], refs[2:4], refs[4:6], refs[6:8]
    three_lo, three_hi, zero, grad_gate, grad_up, sems = refs[8:]
    n, width = early[0].shape[0], zero.shape[2]
    fetch, copies = fetcher(sems)
    for ref, tail, dst in zip(early, late, (grad_gate, grad_up)):
        fetch(ref, dst.at[pl.ds(0, n)])
        fetch(tail, dst.at[pl.ds(n, n)])
    waiter(copies)()
    h, extra = three_lo.shape[1], tails[0].shape[1]
    for k in LAST_ORDER:
        at = columns(place, k, width)
        value = grad_product((grad_gate, grad_up), w_gate[at, :], w_up[at, :])
        for kind in range(2):
            part = value[kind * n : (kind + 1) * n]
            if k:
                three_lo[kind] = part[:h]
                three_hi[kind, pl.ds(0, n - h)] = part[h:]
                three_hi[kind, pl.ds(n - h, extra)] = tails[0][kind]
            else:
                zero[kind, pl.ds(0, n)] = part
                zero[kind, pl.ds(n, extra)] = tails[1][kind]


def call(body, name, out_shape, scratch, flops, operands, weights):
    n_bytes = sum(o.size * o.dtype.itemsize for o in operands)
    n_bytes += sum(2 * o.size for o in out_shape)
    return pl.pallas_call(
        body,
        out_shape=out_shape,
        in_specs=[pl.BlockSpec(memory_space=pltpu.SMEM)]
        + [
            pl.BlockSpec(memory_space=pltpu.VMEM if any(o is w for w in weights) else pl.ANY)
            for o in operands[1:]
        ],
        out_specs=[pl.BlockSpec(memory_space=pltpu.VMEM)] * len(out_shape),
        scratch_shapes=scratch,
        compiler_params=pltpu.CompilerParams(vmem_limit_bytes=VMEM_MB[name] * 2**20),
        cost_estimate=pl.CostEstimate(flops=flops, bytes_accessed=n_bytes, transcendentals=0),
        name=name,
    )(*operands)


def shaped(*shape):
    return jax.ShapeDtypeStruct(shape, BF16)


def front_call(place, parts, weights):
    own = parts[0]
    n = own.shape[0] // 2
    model, hidden = weights[0].shape[0], weights[0].shape[1] // 2
    return call(
        front_body,
        "front",
        [shaped(n, 2 * hidden)] * 3,
        [pltpu.VMEM((n, model), BF16)] * 2
        + [pltpu.SemaphoreType.DMA((8,))],
        12 * n * model * hidden,
        (place, *parts, *weights),
        weights,
    )


def middle_call(place, parts, weights, done):
    n, width = parts[0].shape[0] // 2, parts[0].shape[1]
    model, hidden = weights[0].shape[0], weights[0].shape[1] // 2
    far = n * FAR_SHARE[0] // FAR_SHARE[1]
    near = 2 * n - far
    outs = call(
        middle_body,
        "middle",
        [shaped(n, 2 * hidden)] * 2
        + [shaped(4, far, width)] * 2
        + [shaped(2, near, width)]
        + [shaped(2, near // 2, width)] * 2
        + [shaped(2, n - far, width)] * 2,
        [pltpu.VMEM((n, model), BF16)] * 2
        + [pltpu.VMEM((2 * n, 2 * hidden), BF16)] * 3
        + [pltpu.SemaphoreType.DMA((12,))],
        12 * n * model * hidden + 64 * n * width * hidden,
        (place, *parts, *weights, *done),
        weights,
    )
    return outs[:2], outs[2:4], outs[4:7], outs[7:]


def last_call(place, weights, early, late, tails):
    n = early[0].shape[0]
    model, hidden = weights[0].shape[0], weights[0].shape[1] // 2
    width, near = model // 4, n + tails[0].shape[1]
    return call(
        last_body,
        "last",
        [shaped(2, near // 2, width)] * 2 + [shaped(2, near, width)],
        [pltpu.VMEM((2 * n, 2 * hidden), BF16)] * 2
        + [pltpu.SemaphoreType.DMA((4,))],
        32 * n * width * hidden,
        (place, *weights[:2], *early, *late, *tails),
        (*weights[:2], *tails),
    )


def add(*terms):
    return sum(t.astype(F32) for t in terms).astype(BF16)


def turned(step):
    spans = lax.axis_size("x")
    return [
        (c * spans + x, c * spans + (x + (1 - 2 * c) * step) % spans)
        for c in range(2)
        for x in range(spans)
    ]


def ahead(block):
    return lax.ppermute(block, ("c", "x"), turned(1))


def behind(block):
    return lax.ppermute(block, ("c", "x"), turned(-1))


def across(block):
    return lax.ppermute(block, "z", [(0, 1), (1, 0)])


def gather(own):
    n = own.shape[0] // 2
    barrier = lax.optimization_barrier
    partner, a, b = barrier((across(own), ahead(own), behind(own)))
    up = ahead(jnp.concatenate([partner[:n], a[:n]]))
    down = behind(jnp.concatenate([partner[:n], b[n:]]))
    over = across(jnp.concatenate([a[n:], b[n:]]))
    up, down, over = barrier((up, down, over))
    last = (ahead(up[: n // 2]), behind(down[n // 2 : n]), across(down[n:]))
    return (own, a, b, up, down), (partner, up, down, over, *last)


def shards(tokens, cotangent, expert_ids, gate_probs, w_gate, w_up, w_down):
    n_experts = lax.axis_size("e")
    count, top = expert_ids.shape
    width = tokens.shape[1]
    capacity = (5 * count * top + 4 * n_experts - 1) // (4 * n_experts)
    slots = n_experts * capacity

    mine = (w_gate, w_up, w_down)
    other = tuple(lax.ppermute(w, "c", [(0, 1), (1, 0)]) for w in mine)
    place = jnp.stack(
        [lax.axis_index("z"), lax.axis_index("x"), 1 - 2 * lax.axis_index("c")]
    ).astype(jnp.int32)

    flat_ids = expert_ids.T.reshape(-1)
    onehot = (flat_ids[:, None] == jnp.arange(n_experts, dtype=jnp.int32)[None, :]).astype(
        jnp.int32
    )
    before = jnp.cumsum(onehot, axis=0) - onehot
    slot_ids = jnp.sum(before * onehot, axis=1)
    position = jnp.where(slot_ids < capacity, flat_ids * capacity + slot_ids, slots)
    hit = jnp.arange(slots, dtype=jnp.int32)[:, None] == position[None, :]
    pick = [hit[:, k * count : (k + 1) * count] for k in range(top)]
    any_pick = functools.reduce(jnp.logical_or, pick).astype(BF16)
    row_gate = jnp.sum(jnp.where(hit, gate_probs.T.reshape(-1)[None, :], 0.0), axis=1)
    token_rows = jnp.dot(any_pick, tokens, preferred_element_type=F32).astype(BF16)
    scaled_rows = (
        jnp.dot(any_pick, cotangent, preferred_element_type=F32) * row_gate[:, None]
    ).astype(BF16)

    shape = (n_experts, 1, capacity, width)
    send = jnp.concatenate([token_rows.reshape(shape), scaled_rows.reshape(shape)], axis=1)

    def exchange(block):
        return lax.all_to_all(block, "e", split_axis=0, concat_axis=0, tiled=True)

    own, *other = lax.optimization_barrier((exchange(send), *other))
    own = own.transpose(1, 0, 2, 3).reshape(2 * slots, width)
    weights = [jnp.concatenate([a, b], axis) for a, b, axis in zip(mine, other, (1, 1, 0))]
    near_parts, far_parts = gather(own)
    done = front_call(place, near_parts, weights)
    late, (my_out, their_out), (up_1, one_lo, two_hi), tails = middle_call(
        place, far_parts, weights, done
    )
    got, up_in, two_down = across(their_out), ahead(up_1), behind(two_hi)
    three_lo, three_hi, zero = last_call(place, weights, done[1:], late, tails)
    three_down = behind(three_lo)
    h, f = one_lo.shape[1], my_out.shape[1] // 2
    two_up, one_up = up_in[:, :h], up_in[:, h:]
    rest_up, rest_down = ahead(add(one_lo, two_up)), behind(add(three_hi, two_down))
    near_lo = [add(zero[i, :h], rest_up[i], three_down[i]) for i in range(2)]
    near_hi = [add(zero[i, h:], one_up[i], rest_down[i]) for i in range(2)]
    near_in = across(jnp.concatenate([near_lo[1], near_hi[1]]))
    sum_two, sum_one, sum_three, sum_zero = (add(my_out[j], got[j]) for j in range(4))
    far_up = ahead(jnp.concatenate([sum_two[:f], sum_one[f:]]))
    far_down = behind(jnp.concatenate([sum_three[:f], sum_two[f:]]))
    far_rest_up = ahead(add(sum_one[:f], far_up[:f]))
    far_rest_down = behind(add(sum_three[f:], far_down[f:]))
    far_lo = add(sum_zero[:f], far_rest_up, far_down[:f])
    far_hi = add(sum_zero[f:], far_up[f:], far_rest_down)
    near_total = add(jnp.concatenate([near_lo[0], near_hi[0]]), near_in)
    grad_total = near_total[:slots]
    out_total = jnp.concatenate([far_lo, far_hi, near_total[slots:]])
    total = jnp.concatenate([out_total.reshape(shape), grad_total.reshape(shape)], axis=1)
    back = exchange(total)
    out_rows = back[:, 0].reshape(slots, width)
    grad_rows = back[:, 1].reshape(slots, width)

    out_add = 0.0
    for k in range(top):
        picked = lax.dot_general(
            pick[k].astype(BF16),
            out_rows,
            (((0,), (0,)), ((), ())),
            preferred_element_type=F32,
        )
        out_add = out_add + gate_probs[:, k : k + 1] * picked
    grad_add = lax.dot_general(
        any_pick, grad_rows, (((0,), (0,)), ((), ())), preferred_element_type=F32
    )
    mixed = (tokens.astype(F32) + out_add).astype(BF16)
    token_grad = (cotangent.astype(F32) + grad_add).astype(BF16)
    return (mixed, token_grad)


def solution(mesh):
    n_expert, n_tensor = mesh.devices.shape
    fine = Mesh(mesh.devices.reshape(n_expert // 4, 2, 2, n_tensor), ("e", "z", "c", "x"))
    shard = ("e", "z", "c")
    everywhere = ("e", "z", "c", "x")
    placed = (
        P(shard, "x"),
        P(shard, "x"),
        P(shard, None),
        P(shard, None),
        P(None, everywhere),
        P(None, everywhere),
        P(everywhere, None),
    )
    return jax.shard_map(
        shards,
        mesh=fine,
        in_specs=placed,
        out_specs=(P(shard, "x"), P(shard, "x")),
        check_vma=False,
    )
```

```python
import functools

import jax
import jax.numpy as jnp
from jax import lax
from jax.experimental import pallas as pl
from jax.experimental.pallas import tpu as pltpu
from jax.sharding import Mesh, PartitionSpec as P

F32 = jnp.float32
BF16 = jnp.bfloat16
CONTRACT_LAST = (((1,), (1,)), ((), ()))
HIDDEN_TILE = 256
VMEM_MB = dict(front=6, middle=13, last=7)
OUT_ORDER = (2, 1, 3, 0)
FAR_SHARE = (16, 20)
LAST_ORDER = (1, 3, 0)


def geglu(gate, up, back):
    root = 0.7978845608028654
    cubic = 0.044715
    square = gate * gate
    tanh = jnp.tanh(gate * (root + root * cubic * square))
    half = 0.5 * (1.0 + tanh)
    value = gate * half
    slope = half + 0.5 * gate * (1.0 - tanh * tanh) * (root + 3.0 * root * cubic * square)
    return (
        (value * up).astype(BF16),
        (slope * (back * up)).astype(BF16),
        (value * back).astype(BF16),
    )


def fetcher(sems):
    copies = []

    def fetch(src, dst):
        copy = pltpu.make_async_copy(src, dst, sems.at[len(copies)])
        copy.start()
        copies.append(copy)
        return copy

    return fetch, copies


def columns(place, k, width):
    spans = 4
    span = lax.rem(place[1] + place[2] * k + 2 * spans, spans)
    return pl.ds(pl.multiple_of(span * width, 128), width)


def fetch_rows(place, pieces, dst, fetch):
    return [
        fetch(
            ref.at[pl.ds(row, count)],
            dst.at[pl.ds(to, count), columns(place, k, ref.shape[1])],
        )
        for ref, row, count, k, to in pieces
    ]


def front(tok, sca, weights, acts, row, waits):
    w_gate, w_up, w_down = weights
    tile = HIDDEN_TILE
    rows = pl.ds(row, tok.shape[0])

    def hidden_tile(i, carry):
        at = pl.ds(pl.multiple_of(i * tile, tile), tile)
        gate = jnp.dot(tok[...], w_gate[:, at], preferred_element_type=F32)
        up = jnp.dot(tok[...], w_up[:, at], preferred_element_type=F32)
        back = lax.dot_general(sca[...], w_down[at, :], CONTRACT_LAST, preferred_element_type=F32)
        for ref, value in zip(acts, geglu(gate, up, back)):
            ref[rows, at] = value
        return carry

    for wait in waits:
        wait()
    lax.fori_loop(0, w_gate.shape[1] // tile, hidden_tile, 0)


def grad_product(grads, gate_rows, up_rows):
    total = lax.dot_general(
        grads[0][...], gate_rows, CONTRACT_LAST, preferred_element_type=F32
    )
    total += lax.dot_general(grads[1][...], up_rows, CONTRACT_LAST, preferred_element_type=F32)
    return total.astype(BF16)


def waiter(copies):
    def wait():
        for copy in copies:
            copy.wait()

    return wait


def front_body(place, *refs):
    own, behind_1, ahead_1, up, down = refs[:5]
    held, outs = refs[5:8], refs[8:11]
    tok, sca, in_sem = refs[11:]
    n = tok.shape[0]
    fetch, _ = fetcher(in_sem)
    toks = [(own, 0, n, 0, 0), (behind_1, 0, n, 3, 0), (ahead_1, 0, n, 1, 0), (up, n, n, 2, 0)]
    scas = [(own, n, n, 0, 0), (behind_1, n, n, 3, 0), (ahead_1, n, n, 1, 0), (down, n, n, 2, 0)]
    copies = fetch_rows(place, toks, tok, fetch) + fetch_rows(place, scas, sca, fetch)
    front(tok, sca, held, outs, 0, [waiter(copies)])


def middle_body(place, *refs):
    partner, up, down, over, last_up, last_down, last_over = refs[:7]
    held, done, outs = refs[7:10], refs[10:13], refs[13:-6]
    w_gate, w_up, w_down = held
    tok, sca, act, grad_gate, grad_up, in_sem = refs[-6:]
    n, width = tok.shape[0], partner.shape[1]
    acts = (act, grad_gate, grad_up)
    fetch, _ = fetcher(in_sem)
    toks = [(partner, 0, n, 0, 0), (up, 0, n, 3, 0), (down, 0, n, 1, 0)]
    toks += [(last_up, 0, n // 2, 2, 0), (last_down, 0, n // 2, 2, n // 2)]
    scas = [(partner, n, n, 0, 0), (over, 0, n, 3, 0), (over, n, n, 1, 0), (last_over, 0, n, 2, 0)]
    copies = fetch_rows(place, toks, tok, fetch) + fetch_rows(place, scas, sca, fetch)
    acts_in = [fetch(ref, dst.at[pl.ds(0, n)]) for ref, dst in zip(done, acts)]
    front(tok, sca, held, acts, n, [waiter(copies)])
    waiter(acts_in)()
    for ref, out in zip(acts[1:], outs[:2]):
        out[...] = ref[pl.ds(n, n), :]
    mine, theirs, two_lo, two_hi, *tails = outs[2:]
    far, h = mine.shape[1], two_lo.shape[1]
    for j, k in enumerate(OUT_ORDER):
        at = columns(place, k, width)
        value = jnp.dot(act[...], w_down[:, at], preferred_element_type=F32).astype(BF16)
        mine[j] = value[:far]
        theirs[j] = value[n : n + far]
        for kind in range(2):
            tail = value[kind * n + far : (kind + 1) * n]
            if k == 2:
                two_hi[kind, pl.ds(n - h, n - far)] = tail
            else:
                tails[LAST_ORDER.index(k)][kind] = tail
    at = columns(place, 2, width)
    value = grad_product(acts[1:], w_gate[at, :], w_up[at, :])
    for kind in range(2):
        two_lo[kind] = value[kind * n : kind * n + h]
        two_hi[kind, pl.ds(0, n - h)] = value[kind * n + h : (kind + 1) * n]


def last_body(place, *refs):
    w_gate, w_up, early, late, tails = refs[0], refs[1], refs[2:4], refs[4:6], refs[6:9]
    one_lo, one_hi, three_lo, three_hi, zero, grad_gate, grad_up, sems = refs[9:]
    n, width = early[0].shape[0], zero.shape[2]
    fetch, copies = fetcher(sems)
    for ref, tail, dst in zip(early, late, (grad_gate, grad_up)):
        fetch(ref, dst.at[pl.ds(0, n)])
        fetch(tail, dst.at[pl.ds(n, n)])
    waiter(copies)()
    h, extra = one_lo.shape[1], tails[0].shape[1]
    halves = ((one_lo, one_hi), (three_lo, three_hi))
    for j, k in enumerate(LAST_ORDER):
        at = columns(place, k, width)
        value = grad_product((grad_gate, grad_up), w_gate[at, :], w_up[at, :])
        for kind in range(2):
            part = value[kind * n : (kind + 1) * n]
            if k:
                halves[j][0][kind] = part[:h]
                halves[j][1][kind, pl.ds(0, n - h)] = part[h:]
                halves[j][1][kind, pl.ds(n - h, extra)] = tails[j][kind]
            else:
                zero[kind, pl.ds(0, n)] = part
                zero[kind, pl.ds(n, extra)] = tails[j][kind]


def call(body, name, out_shape, scratch, flops, operands, weights):
    n_bytes = sum(o.size * o.dtype.itemsize for o in operands)
    n_bytes += sum(2 * o.size for o in out_shape)
    return pl.pallas_call(
        body,
        out_shape=out_shape,
        in_specs=[pl.BlockSpec(memory_space=pltpu.SMEM)]
        + [
            pl.BlockSpec(memory_space=pltpu.VMEM if any(o is w for w in weights) else pl.ANY)
            for o in operands[1:]
        ],
        out_specs=[pl.BlockSpec(memory_space=pltpu.VMEM)] * len(out_shape),
        scratch_shapes=scratch,
        compiler_params=pltpu.CompilerParams(vmem_limit_bytes=VMEM_MB[name] * 2**20),
        cost_estimate=pl.CostEstimate(flops=flops, bytes_accessed=n_bytes, transcendentals=0),
        name=name,
    )(*operands)


def shaped(*shape):
    return jax.ShapeDtypeStruct(shape, BF16)


def front_call(place, parts, weights):
    own = parts[0]
    n = own.shape[0] // 2
    model, hidden = weights[0].shape[0], weights[0].shape[1] // 2
    return call(
        front_body,
        "front",
        [shaped(n, 2 * hidden)] * 3,
        [pltpu.VMEM((n, model), BF16)] * 2
        + [pltpu.SemaphoreType.DMA((8,))],
        12 * n * model * hidden,
        (place, *parts, *weights),
        weights,
    )


def middle_call(place, parts, weights, done):
    n, width = parts[0].shape[0] // 2, parts[0].shape[1]
    model, hidden = weights[0].shape[0], weights[0].shape[1] // 2
    far = n * FAR_SHARE[0] // FAR_SHARE[1]
    near = 2 * n - far
    outs = call(
        middle_body,
        "middle",
        [shaped(n, 2 * hidden)] * 2
        + [shaped(4, far, width)] * 2
        + [shaped(2, near // 2, width)] * 2
        + [shaped(2, n - far, width)] * 3,
        [pltpu.VMEM((n, model), BF16)] * 2
        + [pltpu.VMEM((2 * n, 2 * hidden), BF16)] * 3
        + [pltpu.SemaphoreType.DMA((12,))],
        12 * n * model * hidden + 48 * n * width * hidden,
        (place, *parts, *weights, *done),
        weights,
    )
    return outs[:2], outs[2:4], outs[4:6], outs[6:]


def last_call(place, weights, early, late, tails):
    n = early[0].shape[0]
    model, hidden = weights[0].shape[0], weights[0].shape[1] // 2
    width, near = model // 4, n + tails[0].shape[1]
    return call(
        last_body,
        "last",
        [shaped(2, near // 2, width)] * 4 + [shaped(2, near, width)],
        [pltpu.VMEM((2 * n, 2 * hidden), BF16)] * 2
        + [pltpu.SemaphoreType.DMA((4,))],
        48 * n * width * hidden,
        (place, *weights[:2], *early, *late, *tails),
        (*weights[:2], *tails),
    )


def select_body(capacity, *refs):
    given, (send, position), held, sems = refs[:4], refs[4:6], refs[6:10], refs[10]
    fetch, copies = fetcher(sems)
    for src, dst in zip(given, held):
        fetch(src, dst)
    ids, gates, tokens, cotangent = held
    n_experts, (top, count) = send.shape[0], ids.shape
    waiter(copies[:2])()
    slots = n_experts * capacity
    experts = lax.broadcasted_iota(jnp.int32, (n_experts, count), 0)
    earlier = lax.broadcasted_iota(jnp.int32, (count, count), 0) < lax.broadcasted_iota(
        jnp.int32, (count, count), 1
    )
    earlier = jnp.where(earlier, 1.0, 0.0).astype(BF16)
    rows = lax.broadcasted_iota(jnp.int32, (slots, count), 0)
    taken = jnp.zeros((n_experts, 1), F32)
    pick = jnp.zeros((slots, count), F32)
    row_gate = jnp.zeros((slots, 1), F32)
    for k in range(top):
        chosen = ids[pl.ds(k, 1), :]
        onehot = jnp.where(experts == chosen, 1.0, 0.0)
        before = taken + jnp.dot(onehot.astype(BF16), earlier, preferred_element_type=F32)
        slot = jnp.sum(before * onehot, axis=0, keepdims=True).astype(jnp.int32)
        place = jnp.where(slot < capacity, chosen * capacity + slot, slots)
        position[pl.ds(k, 1), :] = place
        hit = rows == place
        pick += jnp.where(hit, 1.0, 0.0)
        row_gate += jnp.sum(jnp.where(hit, gates[pl.ds(k, 1), :], 0.0), axis=1, keepdims=True)
        taken += jnp.sum(onehot, axis=1, keepdims=True)
    pick = pick.astype(BF16)
    waiter(copies[2:])()
    token_rows = jnp.dot(pick, tokens[...], preferred_element_type=F32)
    scaled_rows = row_gate * jnp.dot(pick, cotangent[...], preferred_element_type=F32)
    for e in range(n_experts):
        at = slice(e * capacity, (e + 1) * capacity)
        send[e, 0] = token_rows[at].astype(BF16)
        send[e, 1] = scaled_rows[at].astype(BF16)


def select_call(ids, gates, tokens, cotangent, n_experts, capacity):
    width = tokens.shape[1]
    return pl.pallas_call(
        functools.partial(select_body, capacity),
        out_shape=[
            shaped(n_experts, 2, capacity, width),
            jax.ShapeDtypeStruct(ids.shape, jnp.int32),
        ],
        in_specs=[pl.BlockSpec(memory_space=pltpu.HBM)] * 4,
        out_specs=[pl.BlockSpec(memory_space=pltpu.VMEM)] * 2,
        scratch_shapes=[pltpu.VMEM(a.shape, a.dtype) for a in (ids, gates, tokens, cotangent)]
        + [pltpu.SemaphoreType.DMA((4,))],
        compiler_params=pltpu.CompilerParams(vmem_limit_bytes=60 * 2**20),
        name="select",
    )(ids, gates, tokens, cotangent)


def near_body(zero, rest_up, rest_down, one_up, three_down, _, mine, theirs):
    h = rest_up.shape[1]
    for kind, out in enumerate((mine, theirs)):
        lower = (zero[kind, pl.ds(0, h)], rest_up[kind], three_down[kind])
        upper = (zero[kind, pl.ds(h, h)], one_up[kind], rest_down[kind])
        out[pl.ds(0, h)] = add(*lower)
        out[pl.ds(h, h)] = add(*upper)


def near_call(zero, rest_up, rest_down, one_up, three_down, after):
    whole = pl.BlockSpec(memory_space=pltpu.VMEM)
    return pl.pallas_call(
        near_body,
        out_shape=[shaped(*zero.shape[1:])] * 2,
        in_specs=[whole] * 5 + [pl.BlockSpec(memory_space=pl.ANY)],
        out_specs=[whole] * 2,
        compiler_params=pltpu.CompilerParams(vmem_limit_bytes=12 * 2**20),
        name="near",
    )(zero, rest_up, rest_down, one_up, three_down, after)


def add(*terms):
    return sum(t.astype(F32) for t in terms).astype(BF16)


def turned(step):
    spans = lax.axis_size("x")
    return [
        (c * spans + x, c * spans + (x + (1 - 2 * c) * step) % spans)
        for c in range(2)
        for x in range(spans)
    ]


def ahead(block):
    return lax.ppermute(block, ("c", "x"), turned(1))


def behind(block):
    return lax.ppermute(block, ("c", "x"), turned(-1))


def across(block):
    return lax.ppermute(block, "z", [(0, 1), (1, 0)])


def gather(own):
    n = own.shape[0] // 2
    barrier = lax.optimization_barrier
    partner, a, b = barrier((across(own), ahead(own), behind(own)))
    up = ahead(jnp.concatenate([partner[:n], a[:n]]))
    down = behind(jnp.concatenate([partner[:n], b[n:]]))
    over = across(jnp.concatenate([a[n:], b[n:]]))
    up, down, over = barrier((up, down, over))
    last = (ahead(up[: n // 2]), behind(down[n // 2 : n]), across(down[n:]))
    return (own, a, b, up, down), (partner, up, down, over, *last)


def shards(tokens, cotangent, expert_ids, gate_probs, w_gate, w_up, w_down):
    n_experts = lax.axis_size("e")
    count, top = expert_ids.shape
    width = tokens.shape[1]
    capacity = (5 * count * top + 4 * n_experts - 1) // (4 * n_experts)
    slots = n_experts * capacity

    mine = (w_gate, w_up, w_down)
    other = tuple(lax.ppermute(w, "c", [(0, 1), (1, 0)]) for w in mine)
    place = jnp.stack(
        [lax.axis_index("z"), lax.axis_index("x"), 1 - 2 * lax.axis_index("c")]
    ).astype(jnp.int32)

    send, position = select_call(expert_ids.T, gate_probs.T, tokens, cotangent, n_experts, capacity)
    row_range = jnp.arange(slots, dtype=jnp.int32)[:, None]
    pick = [row_range == position[k][None, :] for k in range(top)]
    any_pick = functools.reduce(jnp.logical_or, pick).astype(BF16)
    shape = (n_experts, 1, capacity, width)

    def exchange(block):
        return lax.all_to_all(block, "e", split_axis=0, concat_axis=0, tiled=True)

    own, *other = lax.optimization_barrier((exchange(send), *other))
    own = own.transpose(1, 0, 2, 3).reshape(2 * slots, width)
    weights = [jnp.concatenate([a, b], axis) for a, b, axis in zip(mine, other, (1, 1, 0))]
    near_parts, far_parts = gather(own)
    done = front_call(place, near_parts, weights)
    late, (my_out, their_out), (two_lo, two_hi), tails = middle_call(
        place, far_parts, weights, done
    )
    got, two_up, two_down = across(their_out), ahead(two_lo), behind(two_hi)
    one_lo, one_hi, three_lo, three_hi, zero = last_call(
        place, weights, done[1:], late, tails
    )
    one_up, three_down = ahead(one_hi), behind(three_lo)
    h, f = one_lo.shape[1], my_out.shape[1] // 2
    rest_up, rest_down = ahead(add(one_lo, two_up)), behind(add(three_hi, two_down))
    sum_two, sum_one, sum_three, sum_zero = (add(my_out[j], got[j]) for j in range(4))
    far_first = jnp.concatenate([sum_three[:f], sum_two[f:]])
    far_up = ahead(jnp.concatenate([sum_two[:f], sum_one[f:]]))
    far_down = behind(far_first)
    near_mine, near_theirs = near_call(zero, rest_up, rest_down, one_up, three_down, far_first)
    near_in = across(near_theirs)
    far_rest_up = ahead(add(sum_one[:f], far_up[:f]))
    far_rest_down = behind(add(sum_three[f:], far_down[f:]))
    far_lo = add(sum_zero[:f], far_rest_up, far_down[:f])
    far_hi = add(sum_zero[f:], far_up[f:], far_rest_down)
    near_total = add(near_mine, near_in)
    grad_total = near_total[:slots]
    out_total = jnp.concatenate([far_lo, far_hi, near_total[slots:]])
    total = jnp.concatenate([out_total.reshape(shape), grad_total.reshape(shape)], axis=1)
    back = exchange(total)
    out_rows = back[:, 0].reshape(slots, width)
    grad_rows = back[:, 1].reshape(slots, width)

    out_add = 0.0
    for k in range(top):
        picked = lax.dot_general(
            pick[k].astype(BF16),
            out_rows,
            (((0,), (0,)), ((), ())),
            preferred_element_type=F32,
        )
        out_add = out_add + gate_probs[:, k : k + 1] * picked
    grad_add = lax.dot_general(
        any_pick, grad_rows, (((0,), (0,)), ((), ())), preferred_element_type=F32
    )
    mixed = (tokens.astype(F32) + out_add).astype(BF16)
    token_grad = (cotangent.astype(F32) + grad_add).astype(BF16)
    return (mixed, token_grad)


def solution(mesh):
    n_expert, n_tensor = mesh.devices.shape
    fine = Mesh(mesh.devices.reshape(n_expert // 4, 2, 2, n_tensor), ("e", "z", "c", "x"))
    shard = ("e", "z", "c")
    everywhere = ("e", "z", "c", "x")
    placed = (
        P(shard, "x"),
        P(shard, "x"),
        P(shard, None),
        P(shard, None),
        P(None, everywhere),
        P(None, everywhere),
        P(everywhere, None),
    )
    return jax.shard_map(
        shards,
        mesh=fine,
        in_specs=placed,
        out_specs=(P(shard, "x"), P(shard, "x")),
        check_vma=False,
    )
```

```python
import functools

import jax
import jax.numpy as jnp
from jax import lax
from jax.experimental import pallas as pl
from jax.experimental.pallas import tpu as pltpu
from jax.sharding import Mesh, PartitionSpec as P

F32 = jnp.float32
BF16 = jnp.bfloat16
CONTRACT_LAST = (((1,), (1,)), ((), ()))
HIDDEN_TILE = 256
VMEM_MB = dict(front=6, middle=13, last=7)
OUT_ORDER = (2, 1, 3, 0)
FAR_SHARE = (16, 20)
LAST_ORDER = (1, 3, 0)


def geglu(gate, up, back):
    root = 0.7978845608028654
    cubic = 0.044715
    square = gate * gate
    tanh = jnp.tanh(gate * (root + root * cubic * square))
    half = 0.5 * (1.0 + tanh)
    value = gate * half
    slope = half + 0.5 * gate * (1.0 - tanh * tanh) * (root + 3.0 * root * cubic * square)
    return (
        (value * up).astype(BF16),
        (slope * (back * up)).astype(BF16),
        (value * back).astype(BF16),
    )


def fetcher(sems):
    copies = []

    def fetch(src, dst):
        copy = pltpu.make_async_copy(src, dst, sems.at[len(copies)])
        copy.start()
        copies.append(copy)
        return copy

    return fetch, copies


def columns(place, k, width):
    spans = 4
    span = lax.rem(place[1] + place[2] * k + 2 * spans, spans)
    return pl.ds(pl.multiple_of(span * width, 128), width)


def fetch_rows(place, pieces, dst, fetch):
    return [
        fetch(
            ref.at[pl.ds(row, count)],
            dst.at[pl.ds(to, count), columns(place, k, ref.shape[1])],
        )
        for ref, row, count, k, to in pieces
    ]


def front(tok, sca, weights, acts, row, waits):
    w_gate, w_up, w_down = weights
    tile = HIDDEN_TILE
    rows = pl.ds(row, tok.shape[0])

    def hidden_tile(i, carry):
        at = pl.ds(pl.multiple_of(i * tile, tile), tile)
        gate = jnp.dot(tok[...], w_gate[:, at], preferred_element_type=F32)
        up = jnp.dot(tok[...], w_up[:, at], preferred_element_type=F32)
        back = lax.dot_general(sca[...], w_down[at, :], CONTRACT_LAST, preferred_element_type=F32)
        for ref, value in zip(acts, geglu(gate, up, back)):
            ref[rows, at] = value
        return carry

    for wait in waits:
        wait()
    lax.fori_loop(0, w_gate.shape[1] // tile, hidden_tile, 0)


def grad_product(grads, gate_rows, up_rows):
    total = lax.dot_general(
        grads[0][...], gate_rows, CONTRACT_LAST, preferred_element_type=F32
    )
    total += lax.dot_general(grads[1][...], up_rows, CONTRACT_LAST, preferred_element_type=F32)
    return total.astype(BF16)


def waiter(copies):
    def wait():
        for copy in copies:
            copy.wait()

    return wait


def front_body(place, *refs):
    own, behind_1, ahead_1, up, down = refs[:5]
    held, outs = refs[5:8], refs[8:11]
    tok, sca, in_sem = refs[11:]
    n = tok.shape[0]
    fetch, _ = fetcher(in_sem)
    toks = [(own, 0, n, 0, 0), (behind_1, 0, n, 3, 0), (ahead_1, 0, n, 1, 0), (up, n, n, 2, 0)]
    scas = [(own, n, n, 0, 0), (behind_1, n, n, 3, 0), (ahead_1, n, n, 1, 0), (down, n, n, 2, 0)]
    copies = fetch_rows(place, toks, tok, fetch) + fetch_rows(place, scas, sca, fetch)
    front(tok, sca, held, outs, 0, [waiter(copies)])


def middle_body(place, *refs):
    partner, up, down, over, last_up, last_over = refs[:6]
    held, done, outs = refs[6:9], refs[9:12], refs[12:-6]
    w_gate, w_up, w_down = held
    tok, sca, act, grad_gate, grad_up, in_sem = refs[-6:]
    n, width = tok.shape[0], partner.shape[1]
    acts = (act, grad_gate, grad_up)
    fetch, _ = fetcher(in_sem)
    toks = [(partner, 0, n, 0, 0), (up, 0, n, 3, 0), (down, 0, n, 1, 0)]
    toks += [(last_up, 0, n, 2, 0)]
    scas = [(partner, n, n, 0, 0), (over, 0, n, 3, 0), (over, n, n, 1, 0), (last_over, 0, n, 2, 0)]
    copies = fetch_rows(place, toks, tok, fetch) + fetch_rows(place, scas, sca, fetch)
    acts_in = [fetch(ref, dst.at[pl.ds(0, n)]) for ref, dst in zip(done, acts)]
    front(tok, sca, held, acts, n, [waiter(copies)])
    waiter(acts_in)()
    for ref, out in zip(acts[1:], outs[:2]):
        out[...] = ref[pl.ds(n, n), :]
    mine, theirs, two_lo, two_hi, *tails = outs[2:]
    far, h = mine.shape[1], two_lo.shape[1]
    for j, k in enumerate(OUT_ORDER):
        at = columns(place, k, width)
        value = jnp.dot(act[...], w_down[:, at], preferred_element_type=F32).astype(BF16)
        mine[j] = value[:far]
        theirs[j] = value[n : n + far]
        for kind in range(2):
            tail = value[kind * n + far : (kind + 1) * n]
            if k == 2:
                two_hi[kind, pl.ds(n - h, n - far)] = tail
            else:
                tails[LAST_ORDER.index(k)][kind] = tail
    at = columns(place, 2, width)
    value = grad_product(acts[1:], w_gate[at, :], w_up[at, :])
    for kind in range(2):
        two_lo[kind] = value[kind * n : kind * n + h]
        two_hi[kind, pl.ds(0, n - h)] = value[kind * n + h : (kind + 1) * n]


def last_body(ks, place, *refs):
    n_in = 6 + len(ks)
    w_gate, w_up, early, late, tails = refs[0], refs[1], refs[2:4], refs[4:6], refs[6:n_in]
    outs, (grad_gate, grad_up, sems) = list(refs[n_in:-3]), refs[-3:]
    n, width = early[0].shape[0], outs[0].shape[2]
    fetch, copies = fetcher(sems)
    for ref, tail, dst in zip(early, late, (grad_gate, grad_up)):
        fetch(ref, dst.at[pl.ds(0, n)])
        fetch(tail, dst.at[pl.ds(n, n)])
    waiter(copies)()
    extra = tails[0].shape[1]
    for k, tail in zip(ks, tails):
        at = columns(place, k, width)
        value = grad_product((grad_gate, grad_up), w_gate[at, :], w_up[at, :])
        lower = outs.pop(0) if k else None
        upper = outs.pop(0)
        h = lower.shape[1] if k else 0
        for kind in range(2):
            part = value[kind * n : (kind + 1) * n]
            if k:
                lower[kind] = part[:h]
            upper[kind, pl.ds(0, n - h)] = part[h:]
            upper[kind, pl.ds(n - h, extra)] = tail[kind]


def call(body, name, out_shape, scratch, flops, operands, weights):
    n_bytes = sum(o.size * o.dtype.itemsize for o in operands)
    n_bytes += sum(2 * o.size for o in out_shape)
    return pl.pallas_call(
        body,
        out_shape=out_shape,
        in_specs=[pl.BlockSpec(memory_space=pltpu.SMEM)]
        + [
            pl.BlockSpec(memory_space=pltpu.VMEM if any(o is w for w in weights) else pl.ANY)
            for o in operands[1:]
        ],
        out_specs=[pl.BlockSpec(memory_space=pltpu.VMEM)] * len(out_shape),
        scratch_shapes=scratch,
        compiler_params=pltpu.CompilerParams(vmem_limit_bytes=VMEM_MB[name] * 2**20),
        cost_estimate=pl.CostEstimate(flops=flops, bytes_accessed=n_bytes, transcendentals=0),
        name=name,
    )(*operands)


def shaped(*shape):
    return jax.ShapeDtypeStruct(shape, BF16)


def front_call(place, parts, weights):
    own = parts[0]
    n = own.shape[0] // 2
    model, hidden = weights[0].shape[0], weights[0].shape[1] // 2
    return call(
        front_body,
        "front",
        [shaped(n, 2 * hidden)] * 3,
        [pltpu.VMEM((n, model), BF16)] * 2
        + [pltpu.SemaphoreType.DMA((8,))],
        12 * n * model * hidden,
        (place, *parts, *weights),
        weights,
    )


def middle_call(place, parts, weights, done):
    n, width = parts[0].shape[0] // 2, parts[0].shape[1]
    model, hidden = weights[0].shape[0], weights[0].shape[1] // 2
    far = n * FAR_SHARE[0] // FAR_SHARE[1]
    near = 2 * n - far
    outs = call(
        middle_body,
        "middle",
        [shaped(n, 2 * hidden)] * 2
        + [shaped(4, far, width)] * 2
        + [shaped(2, near // 2, width)] * 2
        + [shaped(2, n - far, width)] * 3,
        [pltpu.VMEM((n, model), BF16)] * 2
        + [pltpu.VMEM((2 * n, 2 * hidden), BF16)] * 3
        + [pltpu.SemaphoreType.DMA((12,))],
        12 * n * model * hidden + 48 * n * width * hidden,
        (place, *parts, *weights, *done),
        weights,
    )
    return outs[:2], outs[2:4], outs[4:6], outs[6:]


def last_call(place, weights, early, late, ks, tails):
    n = early[0].shape[0]
    model, hidden = weights[0].shape[0], weights[0].shape[1] // 2
    width, near = model // 4, n + tails[0].shape[1]
    outs = []
    for k in ks:
        outs += [shaped(2, near // 2, width)] * 2 if k else [shaped(2, near, width)]
    return call(
        functools.partial(last_body, ks),
        "last",
        outs,
        [pltpu.VMEM((2 * n, 2 * hidden), BF16)] * 2 + [pltpu.SemaphoreType.DMA((4,))],
        16 * len(ks) * n * width * hidden,
        (place, *weights[:2], *early, *late, *tails),
        (*weights[:2], *tails),
    )


def select_body(capacity, *refs):
    given, (send, position), held, sems = refs[:4], refs[4:6], refs[6:10], refs[10]
    fetch, copies = fetcher(sems)
    for src, dst in zip(given, held):
        fetch(src, dst)
    ids, gates, tokens, cotangent = held
    n_experts, (top, count) = send.shape[0], ids.shape
    waiter(copies[:2])()
    slots = n_experts * capacity
    experts = lax.broadcasted_iota(jnp.int32, (n_experts, count), 0)
    earlier = lax.broadcasted_iota(jnp.int32, (count, count), 0) < lax.broadcasted_iota(
        jnp.int32, (count, count), 1
    )
    earlier = jnp.where(earlier, 1.0, 0.0).astype(BF16)
    rows = lax.broadcasted_iota(jnp.int32, (slots, count), 0)
    taken = jnp.zeros((n_experts, 1), F32)
    pick = jnp.zeros((slots, count), F32)
    row_gate = jnp.zeros((slots, 1), F32)
    for k in range(top):
        chosen = ids[pl.ds(k, 1), :]
        onehot = jnp.where(experts == chosen, 1.0, 0.0)
        before = taken + jnp.dot(onehot.astype(BF16), earlier, preferred_element_type=F32)
        slot = jnp.sum(before * onehot, axis=0, keepdims=True).astype(jnp.int32)
        place = jnp.where(slot < capacity, chosen * capacity + slot, slots)
        position[pl.ds(k, 1), :] = place
        hit = rows == place
        pick += jnp.where(hit, 1.0, 0.0)
        row_gate += jnp.sum(jnp.where(hit, gates[pl.ds(k, 1), :], 0.0), axis=1, keepdims=True)
        taken += jnp.sum(onehot, axis=1, keepdims=True)
    pick = pick.astype(BF16)
    waiter(copies[2:])()
    token_rows = jnp.dot(pick, tokens[...], preferred_element_type=F32)
    scaled_rows = row_gate * jnp.dot(pick, cotangent[...], preferred_element_type=F32)
    for e in range(n_experts):
        at = slice(e * capacity, (e + 1) * capacity)
        send[e, 0] = token_rows[at].astype(BF16)
        send[e, 1] = scaled_rows[at].astype(BF16)


def select_call(ids, gates, tokens, cotangent, n_experts, capacity):
    width = tokens.shape[1]
    return pl.pallas_call(
        functools.partial(select_body, capacity),
        out_shape=[
            shaped(n_experts, 2, capacity, width),
            jax.ShapeDtypeStruct(ids.shape, jnp.int32),
        ],
        in_specs=[pl.BlockSpec(memory_space=pltpu.HBM)] * 4,
        out_specs=[pl.BlockSpec(memory_space=pltpu.VMEM)] * 2,
        scratch_shapes=[pltpu.VMEM(a.shape, a.dtype) for a in (ids, gates, tokens, cotangent)]
        + [pltpu.SemaphoreType.DMA((4,))],
        compiler_params=pltpu.CompilerParams(vmem_limit_bytes=60 * 2**20),
        name="select",
    )(ids, gates, tokens, cotangent)


def near_body(zero, rest_up, rest_down, one_up, three_down, _, mine, theirs):
    h = rest_up.shape[1]
    for kind, out in enumerate((mine, theirs)):
        lower = (zero[kind, pl.ds(0, h)], rest_up[kind], three_down[kind])
        upper = (zero[kind, pl.ds(h, h)], one_up[kind], rest_down[kind])
        out[pl.ds(0, h)] = add(*lower)
        out[pl.ds(h, h)] = add(*upper)


def near_call(zero, rest_up, rest_down, one_up, three_down, after):
    whole = pl.BlockSpec(memory_space=pltpu.VMEM)
    return pl.pallas_call(
        near_body,
        out_shape=[shaped(*zero.shape[1:])] * 2,
        in_specs=[whole] * 5 + [pl.BlockSpec(memory_space=pl.ANY)],
        out_specs=[whole] * 2,
        compiler_params=pltpu.CompilerParams(vmem_limit_bytes=12 * 2**20),
        name="near",
    )(zero, rest_up, rest_down, one_up, three_down, after)


def add(*terms):
    return sum(t.astype(F32) for t in terms).astype(BF16)


def turned(step):
    spans = lax.axis_size("x")
    return [
        (c * spans + x, c * spans + (x + (1 - 2 * c) * step) % spans)
        for c in range(2)
        for x in range(spans)
    ]


def ahead(block):
    return lax.ppermute(block, ("c", "x"), turned(1))


def behind(block):
    return lax.ppermute(block, ("c", "x"), turned(-1))


def across(block):
    return lax.ppermute(block, "z", [(0, 1), (1, 0)])


def gather(own):
    n = own.shape[0] // 2
    barrier = lax.optimization_barrier
    partner, a, b = barrier((across(own), ahead(own), behind(own)))
    up = ahead(jnp.concatenate([partner[:n], a[:n]]))
    down = behind(jnp.concatenate([partner[:n], b[n:]]))
    over = across(jnp.concatenate([a[n:], b[n:]]))
    up, down, over = barrier((up, down, over))
    return (own, a, b, up, down), (partner, up, down, over, ahead(up[:n]), across(down[n:]))


def shards(tokens, cotangent, expert_ids, gate_probs, w_gate, w_up, w_down):
    n_experts = lax.axis_size("e")
    count, top = expert_ids.shape
    width = tokens.shape[1]
    capacity = (5 * count * top + 4 * n_experts - 1) // (4 * n_experts)
    slots = n_experts * capacity

    mine = (w_gate, w_up, w_down)
    other = tuple(lax.ppermute(w, "c", [(0, 1), (1, 0)]) for w in mine)
    place = jnp.stack(
        [lax.axis_index("z"), lax.axis_index("x"), 1 - 2 * lax.axis_index("c")]
    ).astype(jnp.int32)

    send, position = select_call(expert_ids.T, gate_probs.T, tokens, cotangent, n_experts, capacity)
    row_range = jnp.arange(slots, dtype=jnp.int32)[:, None]
    pick = [row_range == position[k][None, :] for k in range(top)]
    any_pick = functools.reduce(jnp.logical_or, pick).astype(BF16)
    shape = (n_experts, 1, capacity, width)

    def exchange(block):
        return lax.all_to_all(block, "e", split_axis=0, concat_axis=0, tiled=True)

    own, *other = lax.optimization_barrier((exchange(send), *other))
    own = own.transpose(1, 0, 2, 3).reshape(2 * slots, width)
    weights = [jnp.concatenate([a, b], axis) for a, b, axis in zip(mine, other, (1, 1, 0))]
    near_parts, far_parts = gather(own)
    done = front_call(place, near_parts, weights)
    late, (my_out, their_out), (two_lo, two_hi), tails = middle_call(
        place, far_parts, weights, done
    )
    got, two_up, two_down = across(their_out), ahead(two_lo), behind(two_hi)
    one_lo, one_hi, three_lo, three_hi = last_call(
        place, weights, done[1:], late, LAST_ORDER[:2], tails[:2]
    )
    (zero,) = last_call(place, weights, done[1:], late, LAST_ORDER[2:], tails[2:])
    one_up, three_down = ahead(one_hi), behind(three_lo)
    h, f = one_lo.shape[1], my_out.shape[1] // 2
    rest_up, rest_down = ahead(add(one_lo, two_up)), behind(add(three_hi, two_down))
    sum_two, sum_one, sum_three, sum_zero = (add(my_out[j], got[j]) for j in range(4))
    far_first = jnp.concatenate([sum_three[:f], sum_two[f:]])
    far_up = ahead(jnp.concatenate([sum_two[:f], sum_one[f:]]))
    far_down = behind(far_first)
    near_mine, near_theirs = near_call(zero, rest_up, rest_down, one_up, three_down, far_first)
    near_in = across(near_theirs)
    far_rest_up = ahead(add(sum_one[:f], far_up[:f]))
    far_rest_down = behind(add(sum_three[f:], far_down[f:]))
    far_lo = add(sum_zero[:f], far_rest_up, far_down[:f])
    far_hi = add(sum_zero[f:], far_up[f:], far_rest_down)
    near_total = add(near_mine, near_in)
    grad_total = near_total[:slots]
    out_total = jnp.concatenate([far_lo, far_hi, near_total[slots:]])
    total = jnp.concatenate([out_total.reshape(shape), grad_total.reshape(shape)], axis=1)
    back = exchange(total)
    out_rows = back[:, 0].reshape(slots, width)
    grad_rows = back[:, 1].reshape(slots, width)

    out_add = 0.0
    for k in range(top):
        picked = lax.dot_general(
            pick[k].astype(BF16),
            out_rows,
            (((0,), (0,)), ((), ())),
            preferred_element_type=F32,
        )
        out_add = out_add + gate_probs[:, k : k + 1] * picked
    grad_add = lax.dot_general(
        any_pick, grad_rows, (((0,), (0,)), ((), ())), preferred_element_type=F32
    )
    mixed = (tokens.astype(F32) + out_add).astype(BF16)
    token_grad = (cotangent.astype(F32) + grad_add).astype(BF16)
    return (mixed, token_grad)


def solution(mesh):
    n_expert, n_tensor = mesh.devices.shape
    fine = Mesh(mesh.devices.reshape(n_expert // 4, 2, 2, n_tensor), ("e", "z", "c", "x"))
    shard = ("e", "z", "c")
    everywhere = ("e", "z", "c", "x")
    placed = (
        P(shard, "x"),
        P(shard, "x"),
        P(shard, None),
        P(shard, None),
        P(None, everywhere),
        P(None, everywhere),
        P(everywhere, None),
    )
    return jax.shard_map(
        shards,
        mesh=fine,
        in_specs=placed,
        out_specs=(P(shard, "x"), P(shard, "x")),
        check_vma=False,
    )
```

```python
import functools

import jax
import jax.numpy as jnp
from jax import lax
from jax.experimental import pallas as pl
from jax.experimental.pallas import tpu as pltpu
from jax.sharding import Mesh, PartitionSpec as P

F32 = jnp.float32
BF16 = jnp.bfloat16
CONTRACT_LAST = (((1,), (1,)), ((), ()))
HIDDEN_TILE = 256
VMEM_MB = dict(front=6, middle=13, last=7)
OUT_ORDER = (2, 1, 3, 0)
FAR_SHARE = (16, 20)
LAST_ORDER = (1, 3, 0)


def geglu(gate, up, back):
    root = 0.7978845608028654
    cubic = 0.044715
    square = gate * gate
    tanh = jnp.tanh(gate * (root + root * cubic * square))
    half = 0.5 * (1.0 + tanh)
    value = gate * half
    slope = half + 0.5 * gate * (1.0 - tanh * tanh) * (root + 3.0 * root * cubic * square)
    return (
        (value * up).astype(BF16),
        (slope * (back * up)).astype(BF16),
        (value * back).astype(BF16),
    )


def fetcher(sems):
    copies = []

    def fetch(src, dst):
        copy = pltpu.make_async_copy(src, dst, sems.at[len(copies)])
        copy.start()
        copies.append(copy)
        return copy

    return fetch, copies


def columns(place, k, width):
    spans = 4
    span = lax.rem(place[1] + place[2] * k + 2 * spans, spans)
    return pl.ds(pl.multiple_of(span * width, 128), width)


def fetch_rows(place, pieces, dst, fetch):
    return [
        fetch(
            ref.at[pl.ds(row, count)],
            dst.at[pl.ds(to, count), columns(place, k, ref.shape[1])],
        )
        for ref, row, count, k, to in pieces
    ]


def front(tok, sca, weights, acts, row, waits):
    w_gate, w_up, w_down = weights
    tile = HIDDEN_TILE
    rows = pl.ds(row, tok.shape[0])

    def hidden_tile(i, carry):
        at = pl.ds(pl.multiple_of(i * tile, tile), tile)
        gate = jnp.dot(tok[...], w_gate[:, at], preferred_element_type=F32)
        up = jnp.dot(tok[...], w_up[:, at], preferred_element_type=F32)
        back = lax.dot_general(sca[...], w_down[at, :], CONTRACT_LAST, preferred_element_type=F32)
        for ref, value in zip(acts, geglu(gate, up, back)):
            ref[rows, at] = value
        return carry

    for wait in waits:
        wait()
    lax.fori_loop(0, w_gate.shape[1] // tile, hidden_tile, 0)


def grad_product(grads, gate_rows, up_rows):
    total = lax.dot_general(
        grads[0][...], gate_rows, CONTRACT_LAST, preferred_element_type=F32
    )
    total += lax.dot_general(grads[1][...], up_rows, CONTRACT_LAST, preferred_element_type=F32)
    return total.astype(BF16)


def waiter(copies):
    def wait():
        for copy in copies:
            copy.wait()

    return wait


def front_body(place, *refs):
    own, behind_1, ahead_1, up, down = refs[:5]
    held, outs = refs[5:8], refs[8:11]
    tok, sca, in_sem = refs[11:]
    n = tok.shape[0]
    fetch, _ = fetcher(in_sem)
    toks = [(own, 0, n, 0, 0), (behind_1, 0, n, 3, 0), (ahead_1, 0, n, 1, 0), (up, n, n, 2, 0)]
    scas = [(own, n, n, 0, 0), (behind_1, n, n, 3, 0), (ahead_1, n, n, 1, 0), (down, n, n, 2, 0)]
    copies = fetch_rows(place, toks, tok, fetch) + fetch_rows(place, scas, sca, fetch)
    front(tok, sca, held, outs, 0, [waiter(copies)])


def middle_body(place, *refs):
    partner, up, down, over, last_up, last_over = refs[:6]
    held, done, outs = refs[6:9], refs[9:12], refs[12:-6]
    w_gate, w_up, w_down = held
    tok, sca, act, grad_gate, grad_up, in_sem = refs[-6:]
    n, width = tok.shape[0], partner.shape[1]
    acts = (act, grad_gate, grad_up)
    fetch, _ = fetcher(in_sem)
    toks = [(partner, 0, n, 0, 0), (up, 0, n, 3, 0), (down, 0, n, 1, 0)]
    toks += [(last_up, 0, n, 2, 0)]
    scas = [(partner, n, n, 0, 0), (over, 0, n, 3, 0), (over, n, n, 1, 0), (last_over, 0, n, 2, 0)]
    copies = fetch_rows(place, toks, tok, fetch) + fetch_rows(place, scas, sca, fetch)
    acts_in = [fetch(ref, dst.at[pl.ds(0, n)]) for ref, dst in zip(done, acts)]
    front(tok, sca, held, acts, n, [waiter(copies)])
    waiter(acts_in)()
    for ref, out in zip(acts[1:], outs[:2]):
        out[...] = ref[pl.ds(n, n), :]
    mine, theirs, two_lo, two_hi, *tails = outs[2:]
    far, h = mine.shape[1], two_lo.shape[1]
    for j, k in enumerate(OUT_ORDER):
        at = columns(place, k, width)
        value = jnp.dot(act[...], w_down[:, at], preferred_element_type=F32).astype(BF16)
        mine[j] = value[:far]
        theirs[j] = value[n : n + far]
        for kind in range(2):
            tail = value[kind * n + far : (kind + 1) * n]
            if k == 2:
                two_hi[kind, pl.ds(n - h, n - far)] = tail
            else:
                tails[LAST_ORDER.index(k)][kind] = tail
    at = columns(place, 2, width)
    value = grad_product(acts[1:], w_gate[at, :], w_up[at, :])
    for kind in range(2):
        two_lo[kind] = value[kind * n : kind * n + h]
        two_hi[kind, pl.ds(0, n - h)] = value[kind * n + h : (kind + 1) * n]


def last_body(ks, place, *refs):
    n_in = 6 + len(ks)
    w_gate, w_up, early, late, tails = refs[0], refs[1], refs[2:4], refs[4:6], refs[6:n_in]
    outs, (grad_gate, grad_up, sems) = list(refs[n_in:-3]), refs[-3:]
    n, width = early[0].shape[0], outs[0].shape[2]
    fetch, copies = fetcher(sems)
    for ref, tail, dst in zip(early, late, (grad_gate, grad_up)):
        fetch(ref, dst.at[pl.ds(0, n)])
        fetch(tail, dst.at[pl.ds(n, n)])
    waiter(copies)()
    extra = tails[0].shape[1]
    for k, tail in zip(ks, tails):
        at = columns(place, k, width)
        value = grad_product((grad_gate, grad_up), w_gate[at, :], w_up[at, :])
        lower = outs.pop(0) if k else None
        upper = outs.pop(0)
        h = lower.shape[1] if k else 0
        for kind in range(2):
            part = value[kind * n : (kind + 1) * n]
            if k:
                lower[kind] = part[:h]
            upper[kind, pl.ds(0, n - h)] = part[h:]
            upper[kind, pl.ds(n - h, extra)] = tail[kind]


def call(body, name, out_shape, scratch, flops, operands, weights):
    n_bytes = sum(o.size * o.dtype.itemsize for o in operands)
    n_bytes += sum(2 * o.size for o in out_shape)
    return pl.pallas_call(
        body,
        out_shape=out_shape,
        in_specs=[pl.BlockSpec(memory_space=pltpu.SMEM)]
        + [
            pl.BlockSpec(memory_space=pltpu.VMEM if any(o is w for w in weights) else pl.ANY)
            for o in operands[1:]
        ],
        out_specs=[pl.BlockSpec(memory_space=pltpu.VMEM)] * len(out_shape),
        scratch_shapes=scratch,
        compiler_params=pltpu.CompilerParams(vmem_limit_bytes=VMEM_MB[name] * 2**20),
        cost_estimate=pl.CostEstimate(flops=flops, bytes_accessed=n_bytes, transcendentals=0),
        name=name,
    )(*operands)


def shaped(*shape):
    return jax.ShapeDtypeStruct(shape, BF16)


def front_call(place, parts, weights):
    own = parts[0]
    n = own.shape[0] // 2
    model, hidden = weights[0].shape[0], weights[0].shape[1] // 2
    return call(
        front_body,
        "front",
        [shaped(n, 2 * hidden)] * 3,
        [pltpu.VMEM((n, model), BF16)] * 2
        + [pltpu.SemaphoreType.DMA((8,))],
        12 * n * model * hidden,
        (place, *parts, *weights),
        weights,
    )


def middle_call(place, parts, weights, done):
    n, width = parts[0].shape[0] // 2, parts[0].shape[1]
    model, hidden = weights[0].shape[0], weights[0].shape[1] // 2
    far = n * FAR_SHARE[0] // FAR_SHARE[1]
    near = 2 * n - far
    outs = call(
        middle_body,
        "middle",
        [shaped(n, 2 * hidden)] * 2
        + [shaped(4, far, width)] * 2
        + [shaped(2, near // 2, width)] * 2
        + [shaped(2, n - far, width)] * 3,
        [pltpu.VMEM((n, model), BF16)] * 2
        + [pltpu.VMEM((2 * n, 2 * hidden), BF16)] * 3
        + [pltpu.SemaphoreType.DMA((12,))],
        12 * n * model * hidden + 48 * n * width * hidden,
        (place, *parts, *weights, *done),
        weights,
    )
    return outs[:2], outs[2:4], outs[4:6], outs[6:]


def last_call(place, weights, early, late, ks, tails):
    n = early[0].shape[0]
    model, hidden = weights[0].shape[0], weights[0].shape[1] // 2
    width, near = model // 4, n + tails[0].shape[1]
    outs = []
    for k in ks:
        outs += [shaped(2, near // 2, width)] * 2 if k else [shaped(2, near, width)]
    return call(
        functools.partial(last_body, ks),
        "last",
        outs,
        [pltpu.VMEM((2 * n, 2 * hidden), BF16)] * 2 + [pltpu.SemaphoreType.DMA((4,))],
        16 * len(ks) * n * width * hidden,
        (place, *weights[:2], *early, *late, *tails),
        (*weights[:2], *tails),
    )


def select_body(capacity, *refs):
    given, (send, position), held, sems = refs[:4], refs[4:6], refs[6:10], refs[10]
    fetch, copies = fetcher(sems)
    for src, dst in zip(given, held):
        fetch(src, dst)
    ids, gates, tokens, cotangent = held
    n_experts, (top, count) = send.shape[0], ids.shape
    waiter(copies[:2])()
    slots = n_experts * capacity
    experts = lax.broadcasted_iota(jnp.int32, (n_experts, count), 0)
    earlier = lax.broadcasted_iota(jnp.int32, (count, count), 0) < lax.broadcasted_iota(
        jnp.int32, (count, count), 1
    )
    earlier = jnp.where(earlier, 1.0, 0.0).astype(BF16)
    rows = lax.broadcasted_iota(jnp.int32, (slots, count), 0)
    taken = jnp.zeros((n_experts, 1), F32)
    pick = jnp.zeros((slots, count), F32)
    row_gate = jnp.zeros((slots, 1), F32)
    for k in range(top):
        chosen = ids[pl.ds(k, 1), :]
        onehot = jnp.where(experts == chosen, 1.0, 0.0)
        before = taken + jnp.dot(onehot.astype(BF16), earlier, preferred_element_type=F32)
        slot = jnp.sum(before * onehot, axis=0, keepdims=True).astype(jnp.int32)
        place = jnp.where(slot < capacity, chosen * capacity + slot, slots)
        position[pl.ds(k, 1), :] = place
        hit = rows == place
        pick += jnp.where(hit, 1.0, 0.0)
        row_gate += jnp.sum(jnp.where(hit, gates[pl.ds(k, 1), :], 0.0), axis=1, keepdims=True)
        taken += jnp.sum(onehot, axis=1, keepdims=True)
    pick = pick.astype(BF16)
    waiter(copies[2:])()
    token_rows = jnp.dot(pick, tokens[...], preferred_element_type=F32)
    scaled_rows = row_gate * jnp.dot(pick, cotangent[...], preferred_element_type=F32)
    for e in range(n_experts):
        at = slice(e * capacity, (e + 1) * capacity)
        send[e, 0] = token_rows[at].astype(BF16)
        send[e, 1] = scaled_rows[at].astype(BF16)


def select_call(ids, gates, tokens, cotangent, n_experts, capacity):
    width = tokens.shape[1]
    return pl.pallas_call(
        functools.partial(select_body, capacity),
        out_shape=[
            shaped(n_experts, 2, capacity, width),
            jax.ShapeDtypeStruct(ids.shape, jnp.int32),
        ],
        in_specs=[pl.BlockSpec(memory_space=pltpu.HBM)] * 4,
        out_specs=[pl.BlockSpec(memory_space=pltpu.VMEM)] * 2,
        scratch_shapes=[pltpu.VMEM(a.shape, a.dtype) for a in (ids, gates, tokens, cotangent)]
        + [pltpu.SemaphoreType.DMA((4,))],
        compiler_params=pltpu.CompilerParams(vmem_limit_bytes=60 * 2**20),
        name="select",
    )(ids, gates, tokens, cotangent)


def far_body(mine, got, _, up, down, one_lo, three_hi, zero):
    f = one_lo.shape[0]
    lo, hi = pl.ds(0, f), pl.ds(f, f)

    def total(k, at):
        j = OUT_ORDER.index(k)
        return add(mine[j, at], got[j, at])

    up[lo], up[hi] = total(2, lo), total(1, hi)
    down[lo], down[hi] = total(3, lo), total(2, hi)
    one_lo[...], three_hi[...] = total(1, lo), total(3, hi)
    zero[lo], zero[hi] = total(0, lo), total(0, hi)


def far_call(mine, got, after):
    _, far, width = mine.shape
    whole = pl.BlockSpec(memory_space=pltpu.VMEM)
    return pl.pallas_call(
        far_body,
        out_shape=[shaped(far, width)] * 2 + [shaped(far // 2, width)] * 2 + [shaped(far, width)],
        in_specs=[whole] * 2 + [pl.BlockSpec(memory_space=pl.ANY)],
        out_specs=[whole] * 5,
        compiler_params=pltpu.CompilerParams(vmem_limit_bytes=12 * 2**20),
        name="far",
    )(mine, got, after)


def near_body(zero, rest_up, rest_down, one_up, three_down, _, mine, theirs):
    h = rest_up.shape[1]
    for kind, out in enumerate((mine, theirs)):
        lower = (zero[kind, pl.ds(0, h)], rest_up[kind], three_down[kind])
        upper = (zero[kind, pl.ds(h, h)], one_up[kind], rest_down[kind])
        out[pl.ds(0, h)] = add(*lower)
        out[pl.ds(h, h)] = add(*upper)


def near_call(zero, rest_up, rest_down, one_up, three_down, after):
    whole = pl.BlockSpec(memory_space=pltpu.VMEM)
    return pl.pallas_call(
        near_body,
        out_shape=[shaped(*zero.shape[1:])] * 2,
        in_specs=[whole] * 5 + [pl.BlockSpec(memory_space=pl.ANY)],
        out_specs=[whole] * 2,
        compiler_params=pltpu.CompilerParams(vmem_limit_bytes=12 * 2**20),
        name="near",
    )(zero, rest_up, rest_down, one_up, three_down, after)


def add(*terms):
    return sum(t.astype(F32) for t in terms).astype(BF16)


def turned(step):
    spans = lax.axis_size("x")
    return [
        (c * spans + x, c * spans + (x + (1 - 2 * c) * step) % spans)
        for c in range(2)
        for x in range(spans)
    ]


def ahead(block):
    return lax.ppermute(block, ("c", "x"), turned(1))


def behind(block):
    return lax.ppermute(block, ("c", "x"), turned(-1))


def across(block):
    return lax.ppermute(block, "z", [(0, 1), (1, 0)])


def gather(own):
    n = own.shape[0] // 2
    barrier = lax.optimization_barrier
    partner, a, b = barrier((across(own), ahead(own), behind(own)))
    up = ahead(jnp.concatenate([partner[:n], a[:n]]))
    down = behind(jnp.concatenate([partner[:n], b[n:]]))
    over = across(jnp.concatenate([a[n:], b[n:]]))
    up, down, over = barrier((up, down, over))
    return (own, a, b, up, down), (partner, up, down, over, ahead(up[:n]), across(down[n:]))


def shards(tokens, cotangent, expert_ids, gate_probs, w_gate, w_up, w_down):
    n_experts = lax.axis_size("e")
    count, top = expert_ids.shape
    width = tokens.shape[1]
    capacity = (5 * count * top + 4 * n_experts - 1) // (4 * n_experts)
    slots = n_experts * capacity

    mine = (w_gate, w_up, w_down)
    other = tuple(lax.ppermute(w, "c", [(0, 1), (1, 0)]) for w in mine)
    place = jnp.stack(
        [lax.axis_index("z"), lax.axis_index("x"), 1 - 2 * lax.axis_index("c")]
    ).astype(jnp.int32)

    send, position = select_call(expert_ids.T, gate_probs.T, tokens, cotangent, n_experts, capacity)
    row_range = jnp.arange(slots, dtype=jnp.int32)[:, None]
    pick = [row_range == position[k][None, :] for k in range(top)]
    any_pick = functools.reduce(jnp.logical_or, pick).astype(BF16)
    shape = (n_experts, 1, capacity, width)

    def exchange(block):
        return lax.all_to_all(block, "e", split_axis=0, concat_axis=0, tiled=True)

    own, *other = lax.optimization_barrier((exchange(send), *other))
    own = own.transpose(1, 0, 2, 3).reshape(2 * slots, width)
    weights = [jnp.concatenate([a, b], axis) for a, b, axis in zip(mine, other, (1, 1, 0))]
    near_parts, far_parts = gather(own)
    done = front_call(place, near_parts, weights)
    late, (my_out, their_out), (two_lo, two_hi), tails = middle_call(
        place, far_parts, weights, done
    )
    got, two_up, two_down = across(their_out), ahead(two_lo), behind(two_hi)
    one_lo, one_hi, three_lo, three_hi = last_call(
        place, weights, done[1:], late, LAST_ORDER[:2], tails[:2]
    )
    (zero,) = last_call(place, weights, done[1:], late, LAST_ORDER[2:], tails[2:])
    one_up, three_down = ahead(one_hi), behind(three_lo)
    h, f = one_lo.shape[1], my_out.shape[1] // 2
    rest_up, rest_down = ahead(add(one_lo, two_up)), behind(add(three_hi, two_down))
    far_first, far_second, sum_one, sum_three, sum_zero = far_call(my_out, got, zero)
    far_up, far_down = ahead(far_first), behind(far_second)
    near_mine, near_theirs = near_call(zero, rest_up, rest_down, one_up, three_down, far_second)
    near_in = across(near_theirs)
    far_rest_up = ahead(add(sum_one, far_up[:f]))
    far_rest_down = behind(add(sum_three, far_down[f:]))
    far_lo = add(sum_zero[:f], far_rest_up, far_down[:f])
    far_hi = add(sum_zero[f:], far_up[f:], far_rest_down)
    near_total = add(near_mine, near_in)
    grad_total = near_total[:slots]
    out_total = jnp.concatenate([far_lo, far_hi, near_total[slots:]])
    total = jnp.concatenate([out_total.reshape(shape), grad_total.reshape(shape)], axis=1)
    back = exchange(total)
    out_rows = back[:, 0].reshape(slots, width)
    grad_rows = back[:, 1].reshape(slots, width)

    out_add = 0.0
    for k in range(top):
        picked = lax.dot_general(
            pick[k].astype(BF16),
            out_rows,
            (((0,), (0,)), ((), ())),
            preferred_element_type=F32,
        )
        out_add = out_add + gate_probs[:, k : k + 1] * picked
    grad_add = lax.dot_general(
        any_pick, grad_rows, (((0,), (0,)), ((), ())), preferred_element_type=F32
    )
    mixed = (tokens.astype(F32) + out_add).astype(BF16)
    token_grad = (cotangent.astype(F32) + grad_add).astype(BF16)
    return (mixed, token_grad)


def solution(mesh):
    n_expert, n_tensor = mesh.devices.shape
    fine = Mesh(mesh.devices.reshape(n_expert // 4, 2, 2, n_tensor), ("e", "z", "c", "x"))
    shard = ("e", "z", "c")
    everywhere = ("e", "z", "c", "x")
    placed = (
        P(shard, "x"),
        P(shard, "x"),
        P(shard, None),
        P(shard, None),
        P(None, everywhere),
        P(None, everywhere),
        P(everywhere, None),
    )
    return jax.shard_map(
        shards,
        mesh=fine,
        in_specs=placed,
        out_specs=(P(shard, "x"), P(shard, "x")),
        check_vma=False,
    )
```
